32 devices in a mesh: beam: 2 (over x), freq: 8 (over z, y), tm: 2 (over core).
Axes of the slice: x: 2, y: 2, z: 4, core: 2. Of those that a mesh axis runs over, the one named last changes fastest.
Arguments:
- spectra: float32 [4096, 5120], P(('beam', 'freq'), 'tm'), parts along dimension 0, may hold values from -6 to 6
- delays: int32 [11, 2048], replicated, may hold values from 0 to 1024, as said below
- widths: int32 [8], replicated, may hold values from 1 to 128, as said below
Outputs:
- filtered: float32 [8, 4096, 5120], P(None, ('beam', 'freq'), 'tm'), parts along dimension 1
The draws below stay inside these ranges and needn't reach their ends.
There are 2 independent parts, one for each index of `beam`. The reference program is written for one: setup_inputs(seed, part) draws one part's arguments, and reference() takes and returns one part's arrays. A program takes and returns all parts, laid end to end along the dimension named above; an argument that names none is the same for every part. Nothing has to cross between parts.
Inputs may be any that keep to these rules, and one draw needn't show every extreme that they name: delays[l, r] lies in 0 to 2 ** l, and every level l has some entry equal to 2 ** l. The widths include 1 and 128.
All inputs are finite; a program needn't handle non-finite values.
Results may differ from the reference program's by a relative error of at most 0.0003.
Values sent between devices are 32-bit elements; how exact they have to be, the bound alone decides.
No kernel may reach another device: no remote copies, remote signals or barrier semaphores. Data moves between devices by JAX's collectives and lax.ppermute only.
A program may use at most 192 MiB of HBM per device.

```python
import jax
import jax.numpy as jnp
from jax import lax

F = 2048
LEVELS = 11
NW = 8
TAPS = 128
S = 5120


def draw_delays(key, part):
    draw_key, place_key = jax.random.split(jax.random.fold_in(key, 11))
    bounds = (2 ** jnp.arange(LEVELS)).astype(jnp.int32)
    delay_table = jax.random.randint(draw_key, (LEVELS, F), 0, bounds[:, None] + 1)
    column = jax.random.randint(place_key, (LEVELS,), 0, F)
    delay_table = delay_table.at[jnp.arange(LEVELS), column].set(bounds)
    return delay_table.astype(jnp.int32)


def draw_widths(key, part):
    draw_key, place_key = jax.random.split(jax.random.fold_in(key, 23))
    values = jax.random.randint(draw_key, (NW,), 2, TAPS)
    shuffled = jax.random.permutation(place_key, NW)
    values = values.at[shuffled[0]].set(1).at[shuffled[1]].set(TAPS)
    return values.astype(jnp.int32)


def block_levels(key, dims, cuts, low, high):
    loudness = 1.0
    for position, parts in cuts:
        steps = jax.random.uniform(jax.random.fold_in(jax.random.fold_in(key, 6), position), (parts,), jnp.float32, low / len(cuts), high / len(cuts))
        loudness = loudness * jnp.repeat(jnp.exp(steps), dims[position] // parts).reshape((-1,) + (1,) * (len(dims) - 1 - position))
    return loudness


def noise(own_key, extent, width, bound, cuts=(), kind=jnp.bfloat16):
    level = block_levels(own_key, extent, cuts, -0.22, 0.18) if cuts else 1.0
    drawn = jax.random.normal(own_key, extent, jnp.float32) * width * level
    return jnp.minimum(jnp.maximum(drawn, -bound), bound).astype(kind)


def setup_inputs(seed: int = 0, part: int = 0) -> dict:
    arg_keys = jax.random.split(jax.random.key(seed), 4)
    part_keys = jax.random.split(jax.random.fold_in(arg_keys[3], part), 4)
    return {
        "spectra": noise(part_keys[0], (F, S), 1.0, 6.0, ((0, 8), (1, 2)), jnp.float32),
        "delays": draw_delays(jax.random.fold_in(arg_keys[3], 71), part),
        "widths": draw_widths(jax.random.fold_in(arg_keys[3], 71), part),
    }


def delay_level(current, row_shifts, half_rows):
    row_count, out_width = current.shape
    group_count = row_count // (2 * half_rows)
    block_view = current.reshape(group_count, 2, half_rows, out_width)
    padded = jnp.pad(block_view[:, 1], ((0, 0), (0, 0), (0, half_rows)))
    source_rows = jnp.broadcast_to(padded[:, None], (group_count, 2, half_rows, out_width + half_rows))
    source_rows = source_rows.reshape(row_count, out_width + half_rows)
    delayed = jax.vmap(lambda row_data, offset_at: lax.dynamic_slice_in_dim(row_data, offset_at, out_width))(source_rows, row_shifts.astype(jnp.int32))
    summed = block_view[:, 0][:, None] + delayed.reshape(group_count, 2, half_rows, out_width)
    return summed.reshape(row_count, out_width)

def reference(spectra, delays, widths):
    current = spectra
    for tree_level in range(LEVELS):
        current = delay_level(current, delays[tree_level], 2 ** tree_level)
    padded = jnp.pad(current, ((0, 0), (1, TAPS)))
    running = jnp.cumsum(padded, axis=1)

    def filter_one(box_width):
        upper_sum = lax.dynamic_slice_in_dim(running, box_width.astype(jnp.int32), S, 1)
        scaling = 1.0 / jnp.sqrt(box_width.astype(jnp.float32) * F)
        return (upper_sum - running[:, :S]) * scaling
    return lax.map(filter_one, widths)
```

```python
import functools

import jax
import jax.numpy as jnp
from jax import lax
from jax.experimental import pallas as pl
from jax.experimental.pallas import tpu as pltpu
from jax.sharding import PartitionSpec as P

LANES = 128
SUBLANES = 8
TAPS = 128
CHUNKS = 2
VMEM_LIMIT = 48 * 2**20


def lane_gather(block, index):
    return jnp.take_along_axis(block, index, axis=1, mode="promise_in_bounds")


def shift_plan(shifts, level):
    block_choices = max(1, 2**level // LANES)
    whole = jnp.minimum(shifts >> 7, block_choices - 1)
    reach = lax.broadcasted_iota(jnp.int32, shifts.shape, 1) + shifts - (whole << 7)
    return whole, reach & (LANES - 1), reach < LANES


def add_delayed(load_a, load_b, stores, shift_pair, level, in_blocks, out_blocks):
    block_choices = max(1, 2**level // LANES)
    plans = [shift_plan(shifts, level) for shifts in shift_pair]
    bits = block_choices.bit_length() - 1
    wanted = [[(whole & 2**bit) != 0 for bit in range(bits)] for whole, _, _ in plans]
    kept = {}

    def source(side, stage, j):
        if stage == 0:
            side = 0
        key = (side, stage, j)
        if key not in kept:
            if stage == 0:
                kept[key] = load_b(j)
            else:
                step = 2 ** (stage - 1)
                kept[key] = jnp.where(
                    wanted[side][stage - 1],
                    source(side, stage - 1, j + step),
                    source(side, stage - 1, j),
                )
        return kept[key]

    def turned(side, j):
        if j + block_choices > in_blocks:
            return jnp.zeros((SUBLANES, LANES), jnp.float32)
        return lane_gather(source(side, bits, j), plans[side][1])

    held = [turned(side, 0) for side in range(2)]
    for j in range(out_blocks):
        first = load_a(j)
        following = [turned(side, j + 1) for side in range(2)]
        for side in range(2):
            stores[side](j, first + jnp.where(plans[side][2], held[side], following[side]))
        held = following


def column(table_rows, level):
    return jnp.broadcast_to(table_rows[:, level : level + 1], (SUBLANES, LANES))


def block_of(j):
    return slice(j * LANES, (j + 1) * LANES)


def local_tree_kernel(freq_count, chunks, place, spectra, rim, table, *refs):
    rows, span = spectra.shape
    blocks, rim_blocks = span // LANES, rim.shape[1] // LANES
    total = blocks + rim_blocks
    outs, (work, done, in_sem, out_sem) = refs[: freq_count * chunks], refs[freq_count * chunks :]
    mine = place[0]
    loads = [
        pltpu.make_async_copy(
            spectra.at[:, block_of(j)] if j < blocks else rim.at[:, block_of(j - blocks)],
            work.at[j],
            in_sem.at[j],
        )
        for j in range(total)
    ]
    for load in loads:
        load.start()
    for load in loads:
        load.wait()
    levels = rows.bit_length() - 1
    pairs = rows // (2 * SUBLANES)
    for level in range(levels):
        half = 2**level
        last = level == levels - 1

        def step(pair, carry, level=level, half=half, last=last):
            if half < SUBLANES:
                group, member = pair // 4, pair % 4
                member = (member // half) * 2 * half + member % half
                starts = [group * 64 + member + e * half for e in range(2)]
                spots = [pl.ds(start, SUBLANES, stride=SUBLANES) for start in starts]
                from_table = [
                    pl.ds(mine * rows + start, SUBLANES, stride=SUBLANES) for start in starts
                ]
            else:
                tiles = half // SUBLANES
                tile = (pair // tiles) * 2 * tiles + pair % tiles
                starts = [
                    pl.multiple_of((tile + e * tiles) * SUBLANES, SUBLANES) for e in range(2)
                ]
                spots = [pl.ds(start, SUBLANES) for start in starts]
                from_table = [
                    pl.ds(pl.multiple_of(mine * rows + start, SUBLANES), SUBLANES)
                    for start in starts
                ]
            shifts = [column(table[spot, :], level) for spot in from_table]

            def load(e):
                return lambda j: work[j, spots[e], :]

            def store(e):
                def put(j, value):
                    if last:
                        done[spots[e], block_of(j)] = value
                    else:
                        work[j, spots[e], :] = value

                return put

            add_delayed(
                load(0), load(1), [store(0), store(1)], shifts, level, total, blocks if last else total
            )
            return carry

        lax.fori_loop(0, pairs, step, 0)
    share = rows // chunks // freq_count
    stores = []
    for chunk in range(chunks):
        for mask in range(freq_count):
            n = chunk * freq_count + mask
            start = chunk * (rows // chunks) + jnp.bitwise_xor(mine, mask) * share
            stores.append(
                pltpu.make_async_copy(
                    done.at[pl.ds(pl.multiple_of(start, SUBLANES), share), :], outs[n], out_sem.at[n]
                )
            )
    for store in stores:
        store.start()
    for store in stores:
        store.wait()


def local_tree(position, spectra, rim, table, freq_count, chunks):
    rows, span = spectra.shape
    count = freq_count * chunks
    total = (span + rim.shape[1]) // LANES
    share = jax.ShapeDtypeStruct((rows // count, span), jnp.float32)
    hbm = pl.BlockSpec(memory_space=pl.ANY)
    return pl.pallas_call(
        functools.partial(local_tree_kernel, freq_count, chunks),
        out_shape=[share] * count,
        in_specs=[
            pl.BlockSpec(memory_space=pltpu.SMEM),
            hbm,
            hbm,
            pl.BlockSpec(memory_space=pltpu.VMEM),
        ],
        out_specs=[hbm] * count,
        scratch_shapes=[
            pltpu.VMEM((total, rows, LANES), jnp.float32),
            pltpu.VMEM((rows, span), jnp.float32),
            pltpu.SemaphoreType.DMA((total,)),
            pltpu.SemaphoreType.DMA((count,)),
        ],
        compiler_params=pltpu.CompilerParams(vmem_limit_bytes=VMEM_LIMIT),
        cost_estimate=pl.CostEstimate(
            flops=8 * rows * span, bytes_accessed=8 * rows * span, transcendentals=0
        ),
        name="local_tree",
    )(position, spectra, rim, table)


def cross_tree_kernel(rows, chunk, chunks, place, table, rim, *refs):
    freq_count = rim.shape[0]
    parts, outs = refs[:freq_count], refs[freq_count : 2 * freq_count]
    work, done, in_sem, out_sem = refs[2 * freq_count :]
    share, span = parts[0].shape
    rim_span = rim.shape[2]
    blocks = (span + rim_span) // LANES
    mine = place[0]
    loads = []
    for mask in range(freq_count):
        owner = jnp.bitwise_xor(mine, mask)
        loads.append(
            pltpu.make_async_copy(
                parts[mask], work.at[owner, :, pl.ds(0, span)], in_sem.at[0, mask]
            )
        )
        loads.append(
            pltpu.make_async_copy(
                rim.at[mask], work.at[owner, :, pl.ds(span, rim_span)], in_sem.at[1, mask]
            )
        )
    for load in loads:
        load.start()
    for load in loads:
        load.wait()
    base = chunk * (rows // chunks) + mine * share
    levels = freq_count.bit_length() - 1
    tiles = share // SUBLANES
    for bit in range(levels):
        level = rows.bit_length() - 1 + bit
        out_blocks = blocks - 2**level // LANES
        last = bit == levels - 1

        def step(item, carry, bit=bit, level=level, blocks=blocks, out_blocks=out_blocks, last=last):
            pair, tile = item // tiles, item % tiles
            first = (pair // 2**bit) * 2 * 2**bit + pair % 2**bit
            owners = [first, first + 2**bit]
            spot = pl.ds(pl.multiple_of(tile * SUBLANES, SUBLANES), SUBLANES)
            shifts = [
                column(
                    table[
                        pl.ds(
                            pl.multiple_of(owner * rows + base + tile * SUBLANES, SUBLANES), SUBLANES
                        ),
                        :,
                    ],
                    level,
                )
                for owner in owners
            ]

            def load(e):
                return lambda j: work[owners[e], spot, block_of(j)]

            def store(e):
                def put(j, value):
                    if last:
                        done[owners[e], spot, block_of(j)] = value
                    else:
                        work[owners[e], spot, block_of(j)] = value

                return put

            add_delayed(
                load(0), load(1), [store(0), store(1)], shifts, level, blocks, out_blocks
            )
            return carry

        lax.fori_loop(0, freq_count // 2 * tiles, step, 0)
        blocks = out_blocks
    stores = [
        pltpu.make_async_copy(done.at[jnp.bitwise_xor(mine, mask)], outs[mask], out_sem.at[mask])
        for mask in range(freq_count)
    ]
    for store in stores:
        store.start()
    for store in stores:
        store.wait()


def cross_tree(position, table, rim, parts, rows, chunk, chunks):
    freq_count = len(parts)
    share, span = parts[0].shape
    hbm = pl.BlockSpec(memory_space=pl.ANY)
    return pl.pallas_call(
        functools.partial(cross_tree_kernel, rows, chunk, chunks),
        out_shape=[jax.ShapeDtypeStruct((share, span), jnp.float32)] * freq_count,
        in_specs=[pl.BlockSpec(memory_space=pltpu.SMEM), pl.BlockSpec(memory_space=pltpu.VMEM), hbm]
        + [hbm] * freq_count,
        out_specs=[hbm] * freq_count,
        scratch_shapes=[
            pltpu.VMEM((freq_count, share, span + rim.shape[2]), jnp.float32),
            pltpu.VMEM((freq_count, share, span), jnp.float32),
            pltpu.SemaphoreType.DMA((2, freq_count)),
            pltpu.SemaphoreType.DMA((freq_count,)),
        ],
        compiler_params=pltpu.CompilerParams(vmem_limit_bytes=VMEM_LIMIT),
        cost_estimate=pl.CostEstimate(
            flops=4 * freq_count * share * span,
            bytes_accessed=8 * freq_count * share * span,
            transcendentals=0,
        ),
        name="cross_tree",
    )(position, table, rim, *parts)


def filter_kernel(freq_count, chunk, with_base, place, scale, band, rim, *refs):
    parts, refs = refs[:freq_count], refs[freq_count:]
    if with_base:
        refs = refs[1:]
    out, values, wide, taps, results, in_sem, out_sem = refs
    share, span = parts[0].shape
    group = freq_count * share
    blocks = span // LANES
    mine = place[0]
    loads = [pltpu.make_async_copy(band, taps, in_sem.at[2, 0])]
    for mask in range(freq_count):
        owner = jnp.bitwise_xor(mine, mask)
        spot = pl.ds(pl.multiple_of(owner * share, share), share)
        loads.append(
            pltpu.make_async_copy(parts[mask], values.at[spot, pl.ds(0, span)], in_sem.at[0, mask])
        )
        loads.append(
            pltpu.make_async_copy(
                rim.at[mask], values.at[spot, pl.ds(span, LANES)], in_sem.at[1, mask]
            )
        )
    for load in loads:
        load.start()
    for load in loads:
        load.wait()
    for j in range(blocks + 1):
        exact = values[:, block_of(j)]
        high = exact.astype(jnp.bfloat16)
        low = (exact - high.astype(jnp.float32)).astype(jnp.bfloat16)
        for half, value in ((0, high), (1, low)):
            if j < blocks:
                wide[j, :, pl.ds(2 * half * LANES, LANES)] = value
            if j > 0:
                wide[j - 1, :, pl.ds((2 * half + 1) * LANES, LANES)] = value
    filters = out.shape[0]
    per_dot = 2
    copies = {}
    for pair in range(filters // per_dot):
        slot = pair % 2
        if pair >= 2:
            for copy in copies[pair - 2]:
                copy.wait()
        weights = taps[:, pl.ds(pair * per_dot * TAPS, per_dot * TAPS)]
        scales = [scale[pair * per_dot + e] for e in range(per_dot)]

        def step(j, carry, slot=slot, weights=weights, scales=scales):
            product = jnp.dot(wide[j], weights, preferred_element_type=jnp.float32)
            for e in range(per_dot):
                results[slot, e, :, pl.ds(pl.multiple_of(j * LANES, LANES), LANES)] = (
                    product[:, block_of(e)] * scales[e]
                )
            return carry

        lax.fori_loop(0, blocks, step, 0, unroll=4)
        copies[pair] = [
            pltpu.make_async_copy(
                results.at[slot, e],
                out.at[pair * per_dot + e, pl.ds(chunk * group, group), :],
                out_sem.at[slot, e],
            )
            for e in range(per_dot)
        ]
        for copy in copies[pair]:
            copy.start()
    for pair in range(max(0, filters // per_dot - 2), filters // per_dot):
        for copy in copies[pair]:
            copy.wait()


def box_filters(position, scale, band, rim, parts, base, rows, chunk):
    freq_count = len(parts)
    share, span = parts[0].shape
    group = freq_count * share
    filters = scale.shape[0]
    hbm = pl.BlockSpec(memory_space=pl.ANY)
    smem = pl.BlockSpec(memory_space=pltpu.SMEM)
    operands = [position, scale, band, rim, *parts]
    aliases = {}
    if base is not None:
        aliases = {len(operands): 0}
        operands.append(base)
    return pl.pallas_call(
        functools.partial(filter_kernel, freq_count, chunk, base is not None),
        out_shape=jax.ShapeDtypeStruct((filters, rows, span), jnp.float32),
        in_specs=[smem, smem] + [hbm] * (len(operands) - 2),
        out_specs=hbm,
        input_output_aliases=aliases,
        scratch_shapes=[
            pltpu.VMEM((group, span + LANES), jnp.float32),
            pltpu.VMEM((span // LANES, group, 4 * LANES), jnp.bfloat16),
            pltpu.VMEM(band.shape, jnp.bfloat16),
            pltpu.VMEM((2, 2, group, span), jnp.float32),
            pltpu.SemaphoreType.DMA((3, freq_count)),
            pltpu.SemaphoreType.DMA((2, 2)),
        ],
        compiler_params=pltpu.CompilerParams(vmem_limit_bytes=VMEM_LIMIT),
        cost_estimate=pl.CostEstimate(
            flops=8 * group * span * LANES * filters,
            bytes_accessed=4 * group * span * (filters + 1),
            transcendentals=0,
        ),
        name="box_filters",
    )(*operands)


def band_matrix(widths):
    count = widths.shape[0]
    source = lax.broadcasted_iota(jnp.int32, (4 * TAPS, count * TAPS), 0) % (2 * TAPS)
    start = lax.broadcasted_iota(jnp.int32, (4 * TAPS, count * TAPS), 1) % TAPS
    distance = source - start
    reach = jnp.repeat(widths, TAPS)[None, :]
    return ((distance >= 0) & (distance < reach)).astype(jnp.bfloat16)


def passed_along(value, axis, steps):
    count = lax.axis_size(axis)
    initial, last = (max(0, -steps), min(count, count - steps))
    return lax.ppermute(value, axis, [(source, source + steps) for source in range(initial, last)])


def swapped(parts, freq_count):
    order = sorted(range(1, freq_count), key=lambda mask: (-(mask.bit_length()), mask))
    result = [parts[0]] + [None] * (freq_count - 1)
    for mask in order:
        pairs = [(source, source ^ mask) for source in range(freq_count)]
        result[mask] = lax.ppermute(parts[mask], "freq", pairs)
    return result


def by_residues(spectra, delays, widths):
    rows, span = spectra.shape
    freq_count = lax.axis_size("freq")
    channels = rows * freq_count
    position = lax.axis_index("freq").astype(jnp.int32)[None]
    local_rim = -(-(rows - 1) // LANES) * LANES
    rim = passed_along(spectra[:, :local_rim], "tm", -1)
    table = jnp.pad(delays.T, ((0, 0), (0, LANES - delays.shape[0])))
    band = band_matrix(widths)
    scale = 1.0 / jnp.sqrt(widths.astype(jnp.float32) * channels)
    parts = local_tree(position, spectra, rim, table, freq_count, CHUNKS)
    arrived = [
        swapped(parts[chunk * freq_count : (chunk + 1) * freq_count], freq_count)
        for chunk in range(CHUNKS)
    ]
    returned = []
    for chunk in range(CHUNKS):
        leading = jnp.stack([part[:, : channels - rows] for part in arrived[chunk]])
        leading = passed_along(leading, "tm", -1)
        summed = cross_tree(position, table, leading, arrived[chunk], rows, chunk, CHUNKS)
        returned.append(swapped(summed, freq_count))
    result = None
    for chunk in range(CHUNKS):
        leading = jnp.stack([part[:, :LANES] for part in returned[chunk]])
        leading = passed_along(leading, "tm", -1)
        result = box_filters(position, scale, band, leading, returned[chunk], result, rows, chunk)
    return result


def from_partner(value, axis, stride):
    mask = 2**stride
    pairs = [(source, source ^ mask) for source in range(lax.axis_size(axis))]
    return lax.ppermute(value, axis, pairs)


def delay_rows(source_rows, row_shifts, out_width):
    total_width = source_rows.shape[1]
    top_reach = total_width - out_width
    shift_col = row_shifts[:, None]
    low_part = shift_col % top_reach
    result = source_rows
    bit_value = 1
    while bit_value < top_reach:
        width_now = result.shape[1]
        chosen = low_part // bit_value % 2 == 1
        result = jnp.where(chosen, result[:, bit_value:], result[:, : width_now - bit_value])
        bit_value = bit_value * 2
    lower_shift = result[:, :out_width]
    top_shift = source_rows[:, top_reach : top_reach + out_width]
    return jnp.where(shift_col == top_reach, top_shift, lower_shift)


def delay_block(current, row_shifts, half_rows, out_width):
    row_count, total_width = current.shape
    group_count = row_count // (2 * half_rows)
    block_view = current.reshape(group_count, 2, half_rows, total_width)
    source_rows = jnp.broadcast_to(
        block_view[:, 1][:, None], (group_count, 2, half_rows, total_width)
    )
    delayed = delay_rows(source_rows.reshape(row_count, total_width), row_shifts, out_width)
    summed = block_view[:, 0, :, :out_width][:, None] + delayed.reshape(
        group_count, 2, half_rows, out_width
    )
    return summed.reshape(row_count, out_width)


def by_levels(spectra, delays, widths):
    row_count, time_span = spectra.shape
    local_levels = row_count.bit_length() - 1
    freq_count = lax.axis_size("freq")
    cross_levels = freq_count.bit_length() - 1
    position = lax.axis_index("freq")

    def own_shifts(tree_level):
        return lax.dynamic_slice_in_dim(delays[tree_level], position * row_count, row_count)

    current = spectra
    rim_depth = 2**local_levels - 1
    leading = passed_along(current[:, :rim_depth], "tm", -1)
    current = jnp.concatenate([current, leading], axis=1)
    for tree_level in range(local_levels):
        current = delay_block(
            current, own_shifts(tree_level), 2**tree_level, current.shape[1] - 2**tree_level
        )
    for bit_index in range(cross_levels):
        tree_level = local_levels + bit_index
        reach = 2**tree_level
        leading = passed_along(current[:, :reach], "tm", -1)
        own_ext = jnp.concatenate([current, leading], axis=1)
        partner_ext = from_partner(own_ext, "freq", bit_index)
        is_lower = position // 2**bit_index % 2 == 0
        first_term = jnp.where(is_lower, own_ext[:, :time_span], partner_ext[:, :time_span])
        second_source = jnp.where(is_lower, partner_ext, own_ext)
        current = first_term + delay_rows(second_source, own_shifts(tree_level), time_span)
    leading = passed_along(current[:, :TAPS], "tm", -1)
    extended = jnp.concatenate([current, leading], axis=1)
    block_count = time_span // TAPS
    block_view = extended.reshape(row_count, block_count + 1, TAPS)
    paired = jnp.concatenate([block_view[:, :-1], block_view[:, 1:]], axis=2)
    filter_count = widths.shape[0]
    input_pos = lax.broadcasted_iota(jnp.int32, (2 * TAPS, filter_count, TAPS), 0)
    output_pos = lax.broadcasted_iota(jnp.int32, (2 * TAPS, filter_count, TAPS), 2)
    distance = input_pos - output_pos
    box_widths = widths[None, :, None]
    scaling = 1.0 / jnp.sqrt(widths.astype(jnp.float32) * (row_count * freq_count))
    filter_matrix = jnp.where(
        (distance >= 0) & (distance < box_widths), scaling[None, :, None], 0.0
    )
    filter_matrix = filter_matrix.reshape(2 * TAPS, filter_count * TAPS)
    product = jnp.einsum("rbj,jk->rbk", paired, filter_matrix, precision=lax.Precision.HIGHEST)
    product = product.reshape(row_count, block_count, filter_count, TAPS)
    return jnp.transpose(product, (2, 0, 1, 3)).reshape(filter_count, row_count, time_span)


def fits(rows, span, freq_count, levels):
    channels = rows * freq_count
    return (
        rows % 64 == 0
        and LANES <= rows <= 2 * LANES
        and rows & (rows - 1) == 0
        and freq_count & (freq_count - 1) == 0
        and channels == 2**levels
        and rows % (CHUNKS * freq_count * 2 * SUBLANES) == 0
        and span % LANES == 0
        and channels - rows <= span
    )


def local(spectra, delays, widths):
    if fits(*spectra.shape, lax.axis_size("freq"), delays.shape[0]):
        return by_residues(spectra, delays, widths)
    return by_levels(spectra, delays, widths)


def solution(mesh):
    return jax.shard_map(
        local,
        mesh=mesh,
        in_specs=(P(("beam", "freq"), "tm"), P(), P()),
        out_specs=P(None, ("beam", "freq"), "tm"),
        check_vma=False,
    )
```

```python
import functools

import jax
import jax.numpy as jnp
from jax import lax
from jax.experimental import pallas as pl
from jax.experimental.pallas import tpu as pltpu
from jax.sharding import PartitionSpec as P

LANES = 128
SUBLANES = 8
TAPS = 128
VMEM_LIMIT = 48 * 2**20


def lane_gather(block, index):
    return jnp.take_along_axis(block, index, axis=1, mode="promise_in_bounds")


def add_delayed(load_a, load_b, store, shifts, level, in_blocks, out_blocks):
    block_choices = max(1, 2**level // LANES)
    bits = block_choices.bit_length() - 1
    whole = jnp.minimum(shifts >> 7, block_choices - 1)
    reach = lax.broadcasted_iota(jnp.int32, shifts.shape, 1) + shifts - (whole << 7)
    index, stays = reach & (LANES - 1), reach < LANES
    wanted = [(whole & 2**bit) != 0 for bit in range(bits)]
    kept = {}

    def source(stage, j):
        if (stage, j) not in kept:
            if stage == 0:
                kept[stage, j] = load_b(j)
            else:
                later = source(stage - 1, j + 2 ** (stage - 1))
                kept[stage, j] = jnp.where(wanted[stage - 1], later, source(stage - 1, j))
        return kept[stage, j]

    def turned(j):
        if j + block_choices > in_blocks:
            return jnp.zeros((SUBLANES, LANES), jnp.float32)
        return lane_gather(source(bits, j), index)

    held = turned(0)
    for j in range(out_blocks):
        following = turned(j + 1)
        store(j, load_a(j) + jnp.where(stays, held, following))
        held = following


def block_of(j):
    return slice(j * LANES, (j + 1) * LANES)


def spread_shifts(table, spread, rows_at, count, levels):
    per_step = max(n for n in (1, 2, 4) if count % n == 0)

    def step(item, carry):
        for e in range(per_step):
            tile = item * per_step + e
            values = table[pl.ds(pl.multiple_of(rows_at(tile), SUBLANES), SUBLANES), :]
            for n, level in enumerate(levels):
                spread[n, pl.ds(pl.multiple_of(tile * SUBLANES, SUBLANES), SUBLANES), :] = (
                    jnp.broadcast_to(values[:, level : level + 1], (SUBLANES, LANES))
                )
        return carry

    lax.fori_loop(0, count // per_step, step, 0)


def local_tree_kernel(freq_count, place, spectra, rim, table, *refs):
    rows, span = spectra.shape
    levels = rows.bit_length() - 1
    outs, (even, odd, done, spread, in_sem, out_sem) = refs[:freq_count], refs[freq_count:]
    total, out_blocks = even.shape[0], span // LANES
    mine = place[0]
    loads = []
    for j in range(total):
        at = j - out_blocks
        source = rim.at[:, block_of(at)] if at >= 0 else spectra.at[:, block_of(j)]
        loads.append(pltpu.make_async_copy(source, even.at[j], in_sem.at[j]))
    for load in loads:
        load.start()
    spread_shifts(
        table, spread, lambda tile: mine * rows + tile * SUBLANES, rows // SUBLANES, range(levels)
    )
    for load in loads:
        load.wait()
    pairs = rows // (2 * SUBLANES)
    per_step = max(n for n in (1, 2, 4) if pairs % n == 0)
    for level in range(levels - 1):
        half = 2**level
        source, target = (even, odd) if level % 2 == 0 else (odd, even)

        def step(item, carry, level=level, half=half, source=source, target=target):
            for n in range(per_step):
                pair = item * per_step + n
                if half < SUBLANES:
                    group, member = pair // 4, pair % 4
                    start = group * 64 + (member // half) * 2 * half + member % half
                    spots = [
                        pl.ds(start + e * half, SUBLANES, stride=SUBLANES) for e in range(2)
                    ]
                else:
                    tiles = half // SUBLANES
                    tile = (pair // tiles) * 2 * tiles + pair % tiles
                    spots = [
                        pl.ds(pl.multiple_of((tile + e * tiles) * SUBLANES, SUBLANES), SUBLANES)
                        for e in range(2)
                    ]
                for spot in spots:

                    def put(j, value, spot=spot):
                        target[j, spot, :] = value

                    add_delayed(
                        lambda j: source[j, spots[0], :],
                        lambda j: source[j, spots[1], :],
                        put,
                        spread[level, spot, :],
                        level,
                        total,
                        total,
                    )
            return carry

        lax.fori_loop(0, pairs // per_step, step, 0)
    level = levels - 1
    source = even if level % 2 == 0 else odd
    half = freq_count // 2
    share = rows // freq_count
    tiles = share // SUBLANES
    stores = []
    for mask in range(half):
        lower = jnp.bitwise_and(jnp.bitwise_xor(mine, mask), half - 1)
        starts = [lower * share, (lower + half) * share]
        for tile in range(tiles):
            spots = [
                pl.ds(pl.multiple_of(start + tile * SUBLANES, SUBLANES), SUBLANES)
                for start in starts
            ]
            for spot in spots:

                def put(j, value, spot=spot):
                    done[spot, block_of(j)] = value

                add_delayed(
                    lambda j: source[j, spots[0], :],
                    lambda j: source[j, spots[1], :],
                    put,
                    spread[level, spot, :],
                    level,
                    total,
                    out_blocks,
                )
        for n in (mask, mask + half):
            at = pl.multiple_of(jnp.bitwise_xor(mine, n) * share, SUBLANES)
            stores.append(
                pltpu.make_async_copy(done.at[pl.ds(at, share), :], outs[n], out_sem.at[n])
            )
            stores[-1].start()
    for store in stores:
        store.wait()


def local_tree(position, spectra, rim, table, freq_count):
    rows, span = spectra.shape
    total = (span + rim.shape[1]) // LANES
    hbm = pl.BlockSpec(memory_space=pl.ANY)
    return pl.pallas_call(
        functools.partial(local_tree_kernel, freq_count),
        out_shape=[jax.ShapeDtypeStruct((rows // freq_count, span), jnp.float32)] * freq_count,
        in_specs=[
            pl.BlockSpec(memory_space=pltpu.SMEM),
            hbm,
            hbm,
            pl.BlockSpec(memory_space=pltpu.VMEM),
        ],
        out_specs=[hbm] * freq_count,
        scratch_shapes=[
            pltpu.VMEM((total, rows, LANES), jnp.float32),
            pltpu.VMEM((total, rows, LANES), jnp.float32),
            pltpu.VMEM((rows, span), jnp.float32),
            pltpu.VMEM((rows.bit_length() - 1, rows, LANES), jnp.int32),
            pltpu.SemaphoreType.DMA((total,)),
            pltpu.SemaphoreType.DMA((freq_count,)),
        ],
        compiler_params=pltpu.CompilerParams(vmem_limit_bytes=VMEM_LIMIT),
        cost_estimate=pl.CostEstimate(
            flops=8 * rows * span, bytes_accessed=8 * rows * span, transcendentals=0
        ),
        name="local_tree",
    )(position, spectra, rim, table)


def cross_tree_kernel(rows, masks, rim_count, place, table, *refs):
    freq_count = len(masks)
    rims, refs = refs[:rim_count], refs[rim_count:]
    parts, outs = refs[:freq_count], refs[freq_count : 2 * freq_count]
    even, odd, done, spread, in_sem, out_sem = refs[2 * freq_count :]
    share, span = parts[0].shape
    rim_span = rims[0].shape[2]
    blocks = (span + rim_span) // LANES
    mine = place[0]
    loads = [None] * freq_count
    edges = [rim.at[n] for rim in rims for n in range(rim.shape[0])]
    for mask, part, edge in zip(masks, parts, edges):
        spot = pl.ds(pl.multiple_of(jnp.bitwise_xor(mine, mask) * share, SUBLANES), share)
        loads[mask] = [
            pltpu.make_async_copy(part, even.at[spot, pl.ds(0, span)], in_sem.at[0, mask]),
            pltpu.make_async_copy(edge, even.at[spot, pl.ds(span, rim_span)], in_sem.at[1, mask]),
        ]
        for load in loads[mask]:
            load.start()
    first_level = rows.bit_length() - 1
    levels = freq_count.bit_length() - 1
    tiles = share // SUBLANES
    spread_shifts(
        table,
        spread,
        lambda n: (n // tiles) * rows + mine * share + (n % tiles) * SUBLANES,
        freq_count * tiles,
        range(first_level, first_level + levels),
    )
    per_step = 2 if tiles % 2 == 0 else 1
    stores = []
    for bit in range(levels):
        level = first_level + bit
        out_blocks = blocks - 2**level // LANES
        last = bit == levels - 1
        source, target = (even, odd) if bit % 2 == 0 else (odd, even)
        target = done if last else target
        for mask in range(freq_count):
            other = mask + 2**bit
            if mask & 2**bit:
                continue
            if bit == 0:
                for load in loads[mask] + loads[other]:
                    load.wait()
            lower = jnp.bitwise_and(jnp.bitwise_xor(mine, mask), freq_count - 1 - 2**bit)
            starts = [lower * share, (lower + 2**bit) * share]

            def step(item, carry, bit=bit, level=level, blocks=blocks, out_blocks=out_blocks, source=source, target=target, starts=starts):
                for n in range(per_step):
                    at = (item * per_step + n) * SUBLANES
                    spots = [pl.ds(pl.multiple_of(start + at, SUBLANES), SUBLANES) for start in starts]
                    for spot in spots:

                        def put(j, value, spot=spot):
                            target[spot, block_of(j)] = value

                        add_delayed(
                            lambda j: source[spots[0], block_of(j)],
                            lambda j: source[spots[1], block_of(j)],
                            put,
                            spread[bit, spot, :],
                            level,
                            blocks,
                            out_blocks,
                        )
                return carry

            lax.fori_loop(0, tiles // per_step, step, 0)
            if last:
                for n in (mask, other):
                    spot = pl.ds(pl.multiple_of(jnp.bitwise_xor(mine, n) * share, SUBLANES), share)
                    stores.append(pltpu.make_async_copy(done.at[spot, :], outs[n], out_sem.at[n]))
                    stores[-1].start()
        blocks = out_blocks
    for store in stores:
        store.wait()


def cross_tree(position, table, rims, parts, masks, rows):
    freq_count = len(parts)
    share, span = parts[0].shape
    total = span + rims[0].shape[2]
    group = freq_count * share
    hbm = pl.BlockSpec(memory_space=pl.ANY)
    operands = [*rims, *parts]
    return pl.pallas_call(
        functools.partial(cross_tree_kernel, rows, tuple(masks), len(rims)),
        out_shape=[jax.ShapeDtypeStruct((share, span + LANES), jnp.float32)] * freq_count,
        in_specs=[pl.BlockSpec(memory_space=pltpu.SMEM), pl.BlockSpec(memory_space=pltpu.VMEM)]
        + [hbm] * len(operands),
        out_specs=[hbm] * freq_count,
        scratch_shapes=[
            pltpu.VMEM((group, total), jnp.float32),
            pltpu.VMEM((group, total), jnp.float32),
            pltpu.VMEM((group, span + LANES), jnp.float32),
            pltpu.VMEM((freq_count.bit_length() - 1, group, LANES), jnp.int32),
            pltpu.SemaphoreType.DMA((2, freq_count)),
            pltpu.SemaphoreType.DMA((freq_count,)),
        ],
        compiler_params=pltpu.CompilerParams(vmem_limit_bytes=VMEM_LIMIT),
        cost_estimate=pl.CostEstimate(
            flops=4 * group * span, bytes_accessed=8 * group * span, transcendentals=0
        ),
        name="cross_tree",
    )(position, table, *operands)


def filter_kernel(masks, place, widths, scale, earlier, *refs):
    count = len(masks)
    parts = refs[:count]
    out, mark, values, halves, before, whole, results, in_sem, out_sem = refs[-9:]
    mark[...] = jnp.zeros_like(mark)
    share = parts[0].shape[0]
    blocks = out.shape[2] // LANES
    filters = out.shape[0]
    mine = place[0]
    loads = [pltpu.make_async_copy(parts[n], values.at[n], in_sem.at[n]) for n in range(count)]
    for load in loads:
        load.start()
    row = lax.broadcasted_iota(jnp.int32, (2 * LANES, 2 * LANES), 0) & (LANES - 1)
    col = lax.broadcasted_iota(jnp.int32, (2 * LANES, 2 * LANES), 1)
    ones = ((row < col) | (col >= LANES)).astype(jnp.bfloat16)
    per_dot = max(n for n in (1, 2, 3, 4, 5, 6, 7) if (blocks + 1) % n == 0)
    lane = lax.broadcasted_iota(jnp.int32, (SUBLANES, LANES), 1)
    copies = {}
    for n, mask in enumerate(masks):
        slot = n % 2
        loads[n].wait()
        for j in range(blocks + 1):
            exact = values[n, :, block_of(j)]
            high = exact.astype(jnp.bfloat16)
            low = (exact - high.astype(jnp.float32)).astype(jnp.bfloat16)
            halves[j, :, pl.ds(0, LANES)] = high
            halves[j, :, pl.ds(LANES, LANES)] = low
        for item in range((blocks + 1) // per_dot):
            taken = halves[item * per_dot : (item + 1) * per_dot]
            product = jnp.dot(
                taken.reshape(per_dot * share, 2 * LANES), ones, preferred_element_type=jnp.float32
            )
            for e in range(per_dot):
                rows = slice(e * share, (e + 1) * share)
                before[item * per_dot + e] = product[rows, :LANES]
                whole[item * per_dot + e] = product[rows, LANES:]
        if n >= 2:
            for copy in copies[n - 2]:
                copy.wait()

        def step(item, carry, slot=slot):
            which, tile = item // (share // SUBLANES), item % (share // SUBLANES)
            width = widths[which]
            factor = scale[which]
            stays = lane < LANES - width
            at = pl.ds(pl.multiple_of(tile * SUBLANES, SUBLANES), SUBLANES)
            first = before[0, at, :]
            turned = pltpu.roll(first, LANES - width, 1)
            for j in range(blocks):
                second = before[j + 1, at, :]
                following = pltpu.roll(second, LANES - width, 1)
                upper = jnp.where(stays, turned, following + whole[j, at, :])
                results[slot, which, at, block_of(j)] = (upper - first) * factor
                first, turned = second, following
            return carry

        lax.fori_loop(0, filters * share // SUBLANES, step, 0, unroll=8)
        start = pl.multiple_of(jnp.bitwise_xor(mine, mask) * share, SUBLANES)
        copies[n] = [
            pltpu.make_async_copy(
                results.at[slot, which],
                out.at[which, pl.ds(start, share), :],
                out_sem.at[slot, which],
            )
            for which in range(filters)
        ]
        for copy in copies[n]:
            copy.start()
    for n in range(max(0, count - 2), count):
        for copy in copies[n]:
            copy.wait()


def box_filters(position, widths, scale, earlier, masks, parts, result, rows):
    share, reach = parts[0].shape
    span = reach - LANES
    blocks = span // LANES
    count = len(masks)
    filters = scale.shape[0]
    hbm = pl.BlockSpec(memory_space=pl.ANY)
    smem = pl.BlockSpec(memory_space=pltpu.SMEM)
    operands = [position, widths, scale, earlier, *parts]
    aliases = {}
    if result is not None:
        aliases = {len(operands): 0}
        operands.append(result)
    return pl.pallas_call(
        functools.partial(filter_kernel, masks),
        out_shape=[
            jax.ShapeDtypeStruct((filters, rows, span), jnp.float32),
            jax.ShapeDtypeStruct((SUBLANES, LANES), jnp.float32),
        ],
        in_specs=[smem] * 3 + [hbm] * (len(operands) - 3),
        out_specs=[hbm, pl.BlockSpec(memory_space=pltpu.VMEM)],
        input_output_aliases=aliases,
        scratch_shapes=[
            pltpu.VMEM((count, share, reach), jnp.float32),
            pltpu.VMEM((blocks + 1, share, 2 * LANES), jnp.bfloat16),
            pltpu.VMEM((blocks + 1, share, LANES), jnp.float32),
            pltpu.VMEM((blocks + 1, share, LANES), jnp.float32),
            pltpu.VMEM((2, filters, share, span), jnp.float32),
            pltpu.SemaphoreType.DMA((count,)),
            pltpu.SemaphoreType.DMA((2, filters)),
        ],
        compiler_params=pltpu.CompilerParams(vmem_limit_bytes=VMEM_LIMIT),
        cost_estimate=pl.CostEstimate(
            flops=8 * count * share * span * filters,
            bytes_accessed=4 * count * share * span * (filters + 1),
            transcendentals=0,
        ),
        name="box_filters",
    )(*operands)


def passed_along(value, axis, steps):
    count = lax.axis_size(axis)
    initial, last = (max(0, -steps), min(count, count - steps))
    return lax.ppermute(value, axis, [(source, source + steps) for source in range(initial, last)])


def exchanged(part, mask, freq_count):
    pairs = [(source, source ^ mask) for source in range(freq_count)]
    return lax.ppermute(part, "freq", pairs)


def by_residues(spectra, delays, widths):
    rows, span = spectra.shape
    freq_count = lax.axis_size("freq")
    channels = rows * freq_count
    position = lax.axis_index("freq").astype(jnp.int32)[None]
    local_rim = -(-(rows - 1) // LANES) * LANES
    rim = passed_along(spectra[:, :local_rim], "tm", -1)
    table = jnp.pad(delays.T, ((0, 0), (0, LANES - delays.shape[0])))
    scale = 1.0 / jnp.sqrt(widths.astype(jnp.float32) * channels)
    half = freq_count // 2
    near, far = list(range(half)), list(range(half, freq_count))
    early, late = far[: half // 2], far[half // 2 :]
    sent = {}

    def ready(value, *keys):
        for key in keys:
            value, sent[key] = lax.optimization_barrier((value, sent[key]))
        return value

    def swap(name, parts, masks, *keys):
        sent[name, 0] = parts[0]
        for mask in masks:
            sent[name, mask] = exchanged(ready(parts[mask], *keys), mask, freq_count)

    def leading(name, masks, length):
        return passed_along(jnp.stack([sent[name, mask][:, :length] for mask in masks]), "tm", -1)

    parts = local_tree(position, spectra, rim, table, freq_count)
    name = "out"
    swap(name, parts, early + near[1:])
    for before, mask in zip(early, late):
        swap(name, parts, [mask], (name, before))
    rims = [leading(name, masks, channels - rows + LANES) for masks in (near, far)]
    arrived = [sent[name, mask] for mask in near + far]
    summed = cross_tree(position, table, rims, arrived, near + far, rows)
    result = None
    sent["mark"] = jnp.zeros((SUBLANES, LANES), jnp.float32)

    def filters(name, masks):
        nonlocal result
        parts = [sent[name, mask] for mask in masks]
        result, sent["mark"] = box_filters(
            position, widths, scale, sent["mark"], masks, parts, result, rows
        )

    name = "back"
    swap(name, summed, early + near[1:])
    filters(name, near[:1])
    swap(name, summed, late[:1], "mark")
    filters(name, near[1:])
    swap(name, summed, late[1:], "mark")
    filters(name, early)
    filters(name, late)
    return result


def from_partner(value, axis, stride):
    mask = 2**stride
    pairs = [(source, source ^ mask) for source in range(lax.axis_size(axis))]
    return lax.ppermute(value, axis, pairs)


def delay_rows(source_rows, row_shifts, out_width):
    total_width = source_rows.shape[1]
    top_reach = total_width - out_width
    shift_col = row_shifts[:, None]
    low_part = shift_col % top_reach
    result = source_rows
    bit_value = 1
    while bit_value < top_reach:
        width_now = result.shape[1]
        chosen = low_part // bit_value % 2 == 1
        result = jnp.where(chosen, result[:, bit_value:], result[:, : width_now - bit_value])
        bit_value = bit_value * 2
    lower_shift = result[:, :out_width]
    top_shift = source_rows[:, top_reach : top_reach + out_width]
    return jnp.where(shift_col == top_reach, top_shift, lower_shift)


def delay_block(current, row_shifts, half_rows, out_width):
    row_count, total_width = current.shape
    group_count = row_count // (2 * half_rows)
    block_view = current.reshape(group_count, 2, half_rows, total_width)
    source_rows = jnp.broadcast_to(
        block_view[:, 1][:, None], (group_count, 2, half_rows, total_width)
    )
    delayed = delay_rows(source_rows.reshape(row_count, total_width), row_shifts, out_width)
    summed = block_view[:, 0, :, :out_width][:, None] + delayed.reshape(
        group_count, 2, half_rows, out_width
    )
    return summed.reshape(row_count, out_width)


def by_levels(spectra, delays, widths):
    row_count, time_span = spectra.shape
    local_levels = row_count.bit_length() - 1
    freq_count = lax.axis_size("freq")
    cross_levels = freq_count.bit_length() - 1
    position = lax.axis_index("freq")

    def own_shifts(tree_level):
        return lax.dynamic_slice_in_dim(delays[tree_level], position * row_count, row_count)

    current = spectra
    rim_depth = 2**local_levels - 1
    leading = passed_along(current[:, :rim_depth], "tm", -1)
    current = jnp.concatenate([current, leading], axis=1)
    for tree_level in range(local_levels):
        current = delay_block(
            current, own_shifts(tree_level), 2**tree_level, current.shape[1] - 2**tree_level
        )
    for bit_index in range(cross_levels):
        tree_level = local_levels + bit_index
        reach = 2**tree_level
        leading = passed_along(current[:, :reach], "tm", -1)
        own_ext = jnp.concatenate([current, leading], axis=1)
        partner_ext = from_partner(own_ext, "freq", bit_index)
        is_lower = position // 2**bit_index % 2 == 0
        first_term = jnp.where(is_lower, own_ext[:, :time_span], partner_ext[:, :time_span])
        second_source = jnp.where(is_lower, partner_ext, own_ext)
        current = first_term + delay_rows(second_source, own_shifts(tree_level), time_span)
    leading = passed_along(current[:, :TAPS], "tm", -1)
    extended = jnp.concatenate([current, leading], axis=1)
    block_count = time_span // TAPS
    block_view = extended.reshape(row_count, block_count + 1, TAPS)
    paired = jnp.concatenate([block_view[:, :-1], block_view[:, 1:]], axis=2)
    filter_count = widths.shape[0]
    input_pos = lax.broadcasted_iota(jnp.int32, (2 * TAPS, filter_count, TAPS), 0)
    output_pos = lax.broadcasted_iota(jnp.int32, (2 * TAPS, filter_count, TAPS), 2)
    distance = input_pos - output_pos
    box_widths = widths[None, :, None]
    scaling = 1.0 / jnp.sqrt(widths.astype(jnp.float32) * (row_count * freq_count))
    filter_matrix = jnp.where(
        (distance >= 0) & (distance < box_widths), scaling[None, :, None], 0.0
    )
    filter_matrix = filter_matrix.reshape(2 * TAPS, filter_count * TAPS)
    product = jnp.einsum("rbj,jk->rbk", paired, filter_matrix, precision=lax.Precision.HIGHEST)
    product = product.reshape(row_count, block_count, filter_count, TAPS)
    return jnp.transpose(product, (2, 0, 1, 3)).reshape(filter_count, row_count, time_span)


def fits(rows, span, freq_count, levels):
    channels = rows * freq_count
    return (
        rows % 64 == 0
        and LANES <= rows <= 2 * LANES
        and rows & (rows - 1) == 0
        and freq_count & (freq_count - 1) == 0
        and channels == 2**levels
        and rows % (freq_count * 2 * SUBLANES) == 0
        and freq_count >= 4
        and span % LANES == 0
        and channels - rows + LANES <= span
    )


def local(spectra, delays, widths):
    if fits(*spectra.shape, lax.axis_size("freq"), delays.shape[0]):
        return by_residues(spectra, delays, widths)
    return by_levels(spectra, delays, widths)


def solution(mesh):
    return jax.shard_map(
        local,
        mesh=mesh,
        in_specs=(P(("beam", "freq"), "tm"), P(), P()),
        out_specs=P(None, ("beam", "freq"), "tm"),
        check_vma=False,
    )
```

```python
import functools

import jax
import jax.numpy as jnp
from jax import lax
from jax.experimental import pallas as pl
from jax.experimental.pallas import tpu as pltpu
from jax.sharding import PartitionSpec as P

LANES = 128
SUBLANES = 8
TAPS = 128
LATER = 0.5
LOCAL_VMEM, CROSS_VMEM, FILTER_VMEM = 60 * 2**20, 24 * 2**20, 16 * 2**20


def lane_gather(block, index):
    return jnp.take_along_axis(block, index, axis=1, mode="promise_in_bounds")


def add_delayed(load_a, load_b, store, shifts, level, in_blocks, out_blocks):
    block_choices = max(1, 2**level // LANES)
    bits = block_choices.bit_length() - 1
    whole = jnp.minimum(shifts >> 7, block_choices - 1)
    reach = lax.broadcasted_iota(jnp.int32, shifts.shape, 1) + shifts - (whole << 7)
    index, stays = reach & (LANES - 1), reach < LANES
    wanted = [(whole & 2**bit) != 0 for bit in range(bits)]
    kept = {}

    def source(stage, j):
        if (stage, j) not in kept:
            if stage == 0:
                kept[stage, j] = load_b(j)
            else:
                later = source(stage - 1, j + 2 ** (stage - 1))
                kept[stage, j] = jnp.where(wanted[stage - 1], later, source(stage - 1, j))
        return kept[stage, j]

    def turned(j):
        if j + block_choices > in_blocks:
            return jnp.zeros((SUBLANES, LANES), jnp.float32)
        return lane_gather(source(bits, j), index)

    held = turned(0)
    for j in range(out_blocks):
        following = turned(j + 1)
        store(j, load_a(j) + jnp.where(stays, held, following))
        held = following


def block_of(j):
    return slice(j * LANES, (j + 1) * LANES)


def spread_shifts(table, spread, count, levels):
    per_step = max(n for n in (1, 2, 4) if count % n == 0)

    def step(item, carry):
        for e in range(per_step):
            tile = item * per_step + e
            values = table[pl.ds(pl.multiple_of(tile * SUBLANES, SUBLANES), SUBLANES), :]
            for n, level in enumerate(levels):
                spread[n, pl.ds(pl.multiple_of(tile * SUBLANES, SUBLANES), SUBLANES), :] = (
                    jnp.broadcast_to(values[:, level : level + 1], (SUBLANES, LANES))
                )
        return carry

    lax.fori_loop(0, count // per_step, step, 0)


def views(parts, count, mine, share):
    if len(parts) == 1:
        return [(parts[0], pl.ds(0, count))]
    return [
        (part, pl.ds(pl.multiple_of(jnp.bitwise_xor(mine, mask) * share, SUBLANES), share))
        for mask, part in enumerate(parts)
    ]


def local_tree_kernel(chunks, freq_count, place, spectra, rim, table, *refs):
    rows, span = spectra.shape
    levels = rows.bit_length() - 1
    outs, (even, odd, done, spread, held, in_sem, out_sem) = refs[:-7], refs[-7:]
    total, out_blocks = even.shape[0], span // LANES
    mine = place[0]
    own = table.at[pl.ds(pl.multiple_of(mine * rows, SUBLANES), rows), :]
    shifts = pltpu.make_async_copy(own, held, in_sem.at[total])
    loads = []
    for j in range(total):
        at = j - out_blocks
        source = rim.at[:, block_of(at)] if at >= 0 else spectra.at[:, block_of(j)]
        loads.append(pltpu.make_async_copy(source, even.at[j], in_sem.at[j]))
    for load in [shifts, *loads]:
        load.start()
    shifts.wait()
    spread_shifts(held, spread, rows // SUBLANES, range(levels))
    for load in loads:
        load.wait()
    pairs = rows // (2 * SUBLANES)
    per_step = max(n for n in (1, 2, 4) if pairs % n == 0)
    for level in range(levels):
        half = 2**level
        last = level == levels - 1
        source, target = (even, odd) if level % 2 == 0 else (odd, even)

        def step(item, carry, level=level, half=half, last=last, source=source, target=target):
            for n in range(per_step):
                pair = item * per_step + n
                if half < SUBLANES:
                    group, member = pair // 4, pair % 4
                    start = group * 64 + (member // half) * 2 * half + member % half
                    spots = [
                        pl.ds(start + e * half, SUBLANES, stride=SUBLANES) for e in range(2)
                    ]
                else:
                    tiles = half // SUBLANES
                    tile = (pair // tiles) * 2 * tiles + pair % tiles
                    spots = [
                        pl.ds(pl.multiple_of((tile + e * tiles) * SUBLANES, SUBLANES), SUBLANES)
                        for e in range(2)
                    ]
                for spot in spots:

                    def put(j, value, spot=spot):
                        if last:
                            done[spot, block_of(j)] = value
                        else:
                            target[j, spot, :] = value

                    add_delayed(
                        lambda j: source[j, spots[0], :],
                        lambda j: source[j, spots[1], :],
                        put,
                        spread[level, spot, :],
                        level,
                        total,
                        out_blocks if last else total,
                    )
            return carry

        lax.fori_loop(0, pairs // per_step, step, 0)
    stores = []
    for start, count, parts in chunks:
        targets, outs = outs[:parts], outs[parts:]
        for target, spot in views(targets, count, mine, count // freq_count):
            source = done.at[pl.ds(start, count), :].at[spot, :]
            stores.append(pltpu.make_async_copy(source, target, out_sem.at[len(stores)]))
    for store in stores:
        store.start()
    for store in stores:
        store.wait()


def local_tree(position, spectra, rim, table, chunks, freq_count):
    count = sum(parts for _, _, parts in chunks)
    rows, span = spectra.shape
    total = (span + rim.shape[1]) // LANES
    hbm = pl.BlockSpec(memory_space=pl.ANY)
    return pl.pallas_call(
        functools.partial(local_tree_kernel, tuple(chunks), freq_count),
        out_shape=[
            jax.ShapeDtypeStruct((size // parts, span), jnp.float32)
            for _, size, parts in chunks
            for _ in range(parts)
        ],
        in_specs=[pl.BlockSpec(memory_space=pltpu.SMEM), hbm, hbm, hbm],
        out_specs=[pl.BlockSpec(memory_space=pltpu.HBM)] * count,
        scratch_shapes=[
            pltpu.VMEM((total, rows, LANES), jnp.float32),
            pltpu.VMEM((total, rows, LANES), jnp.float32),
            pltpu.VMEM((rows, span), jnp.float32),
            pltpu.VMEM((rows.bit_length() - 1, rows, LANES), jnp.int32),
            pltpu.VMEM((rows, LANES), jnp.int32),
            pltpu.SemaphoreType.DMA((total + 1,)),
            pltpu.SemaphoreType.DMA((count,)),
        ],
        compiler_params=pltpu.CompilerParams(vmem_limit_bytes=LOCAL_VMEM),
        cost_estimate=pl.CostEstimate(
            flops=8 * rows * span, bytes_accessed=8 * rows * span, transcendentals=0
        ),
        name="local_tree",
    )(position, spectra, rim, table)


def cross_tree_kernel(rows, freq_count, base, count, place, table, rim, *refs):
    parts, outs, refs = refs[:count], refs[count : 2 * count], refs[2 * count :]
    even, odd, done, spread, held, in_sem, out_sem = refs
    group, span = even.shape[0], parts[0].shape[1]
    share = group // freq_count
    blocks = even.shape[1] // LANES
    mine = place[0]
    loads = []
    for owner in range(freq_count):
        start = pl.multiple_of(owner * rows + base + mine * share, SUBLANES)
        spot = pl.ds(owner * share, share)
        loads.append(
            pltpu.make_async_copy(
                table.at[pl.ds(start, share), :], held.at[spot, :], in_sem.at[owner]
            )
        )
    sources = [(0, pair) for pair in views(parts, group, mine, share)]
    edges = [rim] if count == 1 else [rim.at[n] for n in range(count)]
    sources += [(span, pair) for pair in views(edges, group, mine, share)]
    for start, (source, spot) in sources:
        target = even.at[spot, pl.ds(start, source.shape[1])]
        loads.append(pltpu.make_async_copy(source, target, in_sem.at[len(loads)]))
    for load in loads:
        load.start()
    for load in loads[:freq_count]:
        load.wait()
    first_level = rows.bit_length() - 1
    levels = freq_count.bit_length() - 1
    tiles = share // SUBLANES
    spread_shifts(held, spread, freq_count * tiles, range(first_level, first_level + levels))
    for load in loads[freq_count:]:
        load.wait()
    items = freq_count // 2 * tiles
    per_step = 2 if items % 2 == 0 else 1
    for bit in range(levels):
        level = first_level + bit
        out_blocks = blocks - 2**level // LANES
        source, target = (even, odd) if bit % 2 == 0 else (odd, even)
        target = done if bit == levels - 1 else target

        def step(
            item, carry, bit=bit, level=level, blocks=blocks, out_blocks=out_blocks, source=source, target=target
        ):
            for n in range(per_step):
                pair, tile = (item * per_step + n) // tiles, (item * per_step + n) % tiles
                first = (pair // 2**bit) * 2 * 2**bit + pair % 2**bit
                spots = [
                    pl.ds(
                        pl.multiple_of((first + e * 2**bit) * share + tile * SUBLANES, SUBLANES),
                        SUBLANES,
                    )
                    for e in range(2)
                ]
                for spot in spots:

                    def put(j, value, spot=spot):
                        target[spot, block_of(j)] = value

                    add_delayed(
                        lambda j: source[spots[0], block_of(j)],
                        lambda j: source[spots[1], block_of(j)],
                        put,
                        spread[bit, spot, :],
                        level,
                        blocks,
                        out_blocks,
                    )
            return carry

        lax.fori_loop(0, items // per_step, step, 0)
        blocks = out_blocks
    stores = [
        pltpu.make_async_copy(done.at[spot, :], target, out_sem.at[n])
        for n, (target, spot) in enumerate(views(outs, group, mine, share))
    ]
    for store in stores:
        store.start()
    for store in stores:
        store.wait()


def cross_tree(position, table, parts, rim, rows, freq_count, base):
    count = len(parts)
    size, span = parts[0].shape
    group = size * count
    total = span + rim.shape[-1]
    hbm = pl.BlockSpec(memory_space=pl.ANY)
    return pl.pallas_call(
        functools.partial(cross_tree_kernel, rows, freq_count, base, count),
        out_shape=[jax.ShapeDtypeStruct((size, span + LANES), jnp.float32)] * count,
        in_specs=[pl.BlockSpec(memory_space=pltpu.SMEM)] + [hbm] * (2 + count),
        out_specs=[pl.BlockSpec(memory_space=pltpu.HBM if count == 1 else pl.ANY)] * count,
        scratch_shapes=[
            pltpu.VMEM((group, total), jnp.float32),
            pltpu.VMEM((group, total), jnp.float32),
            pltpu.VMEM((group, span + LANES), jnp.float32),
            pltpu.VMEM((freq_count.bit_length() - 1, group, LANES), jnp.int32),
            pltpu.VMEM((group, LANES), jnp.int32),
            pltpu.SemaphoreType.DMA((freq_count + 2 * count,)),
            pltpu.SemaphoreType.DMA((count,)),
        ],
        compiler_params=pltpu.CompilerParams(vmem_limit_bytes=CROSS_VMEM),
        cost_estimate=pl.CostEstimate(
            flops=4 * group * span, bytes_accessed=8 * group * span, transcendentals=0
        ),
        name="cross_tree",
    )(position, table, rim, *parts)


def filter_kernel(base, masks, place, widths, scale, earlier, *refs):
    out, mark, values, halves, before, whole, results, in_sem, out_sem = refs[-9:]
    mark[...] = jnp.zeros_like(mark)
    count, share = values.shape[:2]
    if masks:
        pieces = refs[:count]
        starts = [jnp.bitwise_xor(place[0], mask) * share for mask in masks]
    else:
        pieces = [refs[0].at[pl.ds(n * share, share), :] for n in range(count)]
        starts = [n * share for n in range(count)]
    blocks = out.shape[2] // LANES
    filters = out.shape[0]
    loads = [pltpu.make_async_copy(pieces[n], values.at[n], in_sem.at[n]) for n in range(count)]
    for load in loads:
        load.start()
    row = lax.broadcasted_iota(jnp.int32, (2 * LANES, 2 * LANES), 0) & (LANES - 1)
    col = lax.broadcasted_iota(jnp.int32, (2 * LANES, 2 * LANES), 1)
    ones = ((row < col) | (col >= LANES)).astype(jnp.bfloat16)
    per_dot = max(n for n in (1, 2, 3, 4, 5, 6, 7) if (blocks + 1) % n == 0)
    lane = lax.broadcasted_iota(jnp.int32, (SUBLANES, LANES), 1)
    copies = {}
    for n in range(count):
        slot = n % 2
        loads[n].wait()
        for j in range(blocks + 1):
            exact = values[n, :, block_of(j)]
            high = exact.astype(jnp.bfloat16)
            low = (exact - high.astype(jnp.float32)).astype(jnp.bfloat16)
            halves[j, :, pl.ds(0, LANES)] = high
            halves[j, :, pl.ds(LANES, LANES)] = low
        for item in range((blocks + 1) // per_dot):
            taken = halves[item * per_dot : (item + 1) * per_dot]
            product = jnp.dot(
                taken.reshape(per_dot * share, 2 * LANES), ones, preferred_element_type=jnp.float32
            )
            for e in range(per_dot):
                rows = slice(e * share, (e + 1) * share)
                before[item * per_dot + e] = product[rows, :LANES]
                whole[item * per_dot + e] = product[rows, LANES:]
        if n >= 2:
            for copy in copies[n - 2]:
                copy.wait()

        def step(item, carry, slot=slot):
            which, tile = item // (share // SUBLANES), item % (share // SUBLANES)
            width = widths[which]
            factor = scale[which]
            stays = lane < LANES - width
            at = pl.ds(pl.multiple_of(tile * SUBLANES, SUBLANES), SUBLANES)
            first = before[0, at, :]
            turned = pltpu.roll(first, LANES - width, 1)
            for j in range(blocks):
                second = before[j + 1, at, :]
                following = pltpu.roll(second, LANES - width, 1)
                upper = jnp.where(stays, turned, following + whole[j, at, :])
                results[slot, which, at, block_of(j)] = (upper - first) * factor
                first, turned = second, following
            return carry

        lax.fori_loop(0, filters * share // SUBLANES, step, 0, unroll=8)
        copies[n] = [
            pltpu.make_async_copy(
                results.at[slot, which],
                out.at[which, pl.ds(pl.multiple_of(base + starts[n], SUBLANES), share), :],
                out_sem.at[slot, which],
            )
            for which in range(filters)
        ]
        for copy in copies[n]:
            copy.start()
    for n in range(max(0, count - 2), count):
        for copy in copies[n]:
            copy.wait()


def box_filters(position, widths, scale, earlier, parts, masks, result, rows, base):
    size, reach = parts[0].shape
    share = size if masks else max(n for n in (16, 32) if size % n == 0)
    count = len(parts) * size // share
    span = reach - LANES
    blocks = span // LANES
    filters = scale.shape[0]
    hbm = pl.BlockSpec(memory_space=pl.ANY)
    smem = pl.BlockSpec(memory_space=pltpu.SMEM)
    operands = [position, widths, scale, earlier, *parts]
    aliases = {}
    if result is not None:
        aliases = {len(operands): 0}
        operands.append(result)
    return pl.pallas_call(
        functools.partial(filter_kernel, base, tuple(masks)),
        out_shape=[
            jax.ShapeDtypeStruct((filters, rows, span), jnp.float32),
            jax.ShapeDtypeStruct((SUBLANES, LANES), jnp.float32),
        ],
        in_specs=[smem] * 3 + [hbm] * (len(operands) - 3),
        out_specs=[hbm, pl.BlockSpec(memory_space=pltpu.VMEM)],
        input_output_aliases=aliases,
        scratch_shapes=[
            pltpu.VMEM((count, share, reach), jnp.float32),
            pltpu.VMEM((blocks + 1, share, 2 * LANES), jnp.bfloat16),
            pltpu.VMEM((blocks + 1, share, LANES), jnp.float32),
            pltpu.VMEM((blocks + 1, share, LANES), jnp.float32),
            pltpu.VMEM((2, filters, share, span), jnp.float32),
            pltpu.SemaphoreType.DMA((count,)),
            pltpu.SemaphoreType.DMA((2, filters)),
        ],
        compiler_params=pltpu.CompilerParams(vmem_limit_bytes=FILTER_VMEM),
        cost_estimate=pl.CostEstimate(
            flops=8 * count * share * span * filters,
            bytes_accessed=4 * count * share * span * (filters + 1),
            transcendentals=0,
        ),
        name="box_filters",
    )(*operands)


def passed_along(value, axis, steps):
    count = lax.axis_size(axis)
    initial, last = (max(0, -steps), min(count, count - steps))
    return lax.ppermute(value, axis, [(source, source + steps) for source in range(initial, last)])


def exchanged(parts, freq_count):
    if len(parts) == 1:
        return [lax.all_to_all(parts[0], "freq", 0, 0, tiled=True)]
    result = list(parts)
    for mask in range(1, freq_count):
        pairs = [(source, source ^ mask) for source in range(freq_count)]
        result[mask] = lax.ppermute(parts[mask], "freq", pairs)
    return result


def chunks_of(rows, freq_count):
    tiles = rows // freq_count // SUBLANES
    first = tiles - max(1, int(tiles * LATER))
    counts = [first * SUBLANES * freq_count, (tiles - first) * SUBLANES * freq_count]
    return [(0, counts[0], freq_count), (counts[0], counts[1], 1)]


def by_residues(spectra, delays, widths):
    rows, span = spectra.shape
    freq_count = lax.axis_size("freq")
    channels = rows * freq_count
    position = lax.axis_index("freq").astype(jnp.int32)[None]
    local_rim = -(-(rows - 1) // LANES) * LANES
    rim = passed_along(spectra[:, :local_rim], "tm", -1)
    table = jnp.pad(delays.T, ((0, 0), (0, LANES - delays.shape[0])))
    scale = 1.0 / jnp.sqrt(widths.astype(jnp.float32) * channels)
    reach = channels - rows + LANES
    chunks = chunks_of(rows, freq_count)
    made = local_tree(position, spectra, rim, table, chunks, freq_count)
    arrived = []
    for _, _, count in chunks:
        arrived.append(exchanged(made[:count], freq_count))
        made = made[count:]
    back = []
    for (base, _, count), parts in zip(chunks, arrived):
        edges = [part[:, :reach] for part in parts]
        rim = passed_along(jnp.stack(edges) if count > 1 else edges[0], "tm", -1)
        back.append(cross_tree(position, table, parts, rim, rows, freq_count, base))
    back = [exchanged(parts, freq_count) for parts in back]
    result, mark = None, jnp.zeros((SUBLANES, LANES), jnp.float32)
    half = freq_count // 2
    turns = [(0, range(half)), (1, ()), (0, range(half, freq_count))]
    for chunk, masks in turns:
        base, parts = chunks[chunk][0], back[chunk]
        some = [parts[mask] for mask in masks] or parts
        result, mark = box_filters(
            position, widths, scale, mark, some, tuple(masks), result, rows, base
        )
    return result


def from_partner(value, axis, stride):
    mask = 2**stride
    pairs = [(source, source ^ mask) for source in range(lax.axis_size(axis))]
    return lax.ppermute(value, axis, pairs)


def delay_rows(source_rows, row_shifts, out_width):
    total_width = source_rows.shape[1]
    top_reach = total_width - out_width
    shift_col = row_shifts[:, None]
    low_part = shift_col % top_reach
    result = source_rows
    bit_value = 1
    while bit_value < top_reach:
        width_now = result.shape[1]
        chosen = low_part // bit_value % 2 == 1
        result = jnp.where(chosen, result[:, bit_value:], result[:, : width_now - bit_value])
        bit_value = bit_value * 2
    lower_shift = result[:, :out_width]
    top_shift = source_rows[:, top_reach : top_reach + out_width]
    return jnp.where(shift_col == top_reach, top_shift, lower_shift)


def delay_block(current, row_shifts, half_rows, out_width):
    row_count, total_width = current.shape
    group_count = row_count // (2 * half_rows)
    block_view = current.reshape(group_count, 2, half_rows, total_width)
    source_rows = jnp.broadcast_to(
        block_view[:, 1][:, None], (group_count, 2, half_rows, total_width)
    )
    delayed = delay_rows(source_rows.reshape(row_count, total_width), row_shifts, out_width)
    summed = block_view[:, 0, :, :out_width][:, None] + delayed.reshape(
        group_count, 2, half_rows, out_width
    )
    return summed.reshape(row_count, out_width)


def by_levels(spectra, delays, widths):
    row_count, time_span = spectra.shape
    local_levels = row_count.bit_length() - 1
    freq_count = lax.axis_size("freq")
    cross_levels = freq_count.bit_length() - 1
    position = lax.axis_index("freq")

    def own_shifts(tree_level):
        return lax.dynamic_slice_in_dim(delays[tree_level], position * row_count, row_count)

    current = spectra
    rim_depth = 2**local_levels - 1
    leading = passed_along(current[:, :rim_depth], "tm", -1)
    current = jnp.concatenate([current, leading], axis=1)
    for tree_level in range(local_levels):
        current = delay_block(
            current, own_shifts(tree_level), 2**tree_level, current.shape[1] - 2**tree_level
        )
    for bit_index in range(cross_levels):
        tree_level = local_levels + bit_index
        reach = 2**tree_level
        leading = passed_along(current[:, :reach], "tm", -1)
        own_ext = jnp.concatenate([current, leading], axis=1)
        partner_ext = from_partner(own_ext, "freq", bit_index)
        is_lower = position // 2**bit_index % 2 == 0
        first_term = jnp.where(is_lower, own_ext[:, :time_span], partner_ext[:, :time_span])
        second_source = jnp.where(is_lower, partner_ext, own_ext)
        current = first_term + delay_rows(second_source, own_shifts(tree_level), time_span)
    leading = passed_along(current[:, :TAPS], "tm", -1)
    extended = jnp.concatenate([current, leading], axis=1)
    block_count = time_span // TAPS
    block_view = extended.reshape(row_count, block_count + 1, TAPS)
    paired = jnp.concatenate([block_view[:, :-1], block_view[:, 1:]], axis=2)
    filter_count = widths.shape[0]
    input_pos = lax.broadcasted_iota(jnp.int32, (2 * TAPS, filter_count, TAPS), 0)
    output_pos = lax.broadcasted_iota(jnp.int32, (2 * TAPS, filter_count, TAPS), 2)
    distance = input_pos - output_pos
    box_widths = widths[None, :, None]
    scaling = 1.0 / jnp.sqrt(widths.astype(jnp.float32) * (row_count * freq_count))
    filter_matrix = jnp.where(
        (distance >= 0) & (distance < box_widths), scaling[None, :, None], 0.0
    )
    filter_matrix = filter_matrix.reshape(2 * TAPS, filter_count * TAPS)
    product = jnp.einsum("rbj,jk->rbk", paired, filter_matrix, precision=lax.Precision.HIGHEST)
    product = product.reshape(row_count, block_count, filter_count, TAPS)
    return jnp.transpose(product, (2, 0, 1, 3)).reshape(filter_count, row_count, time_span)


def fits(rows, span, freq_count, levels):
    channels = rows * freq_count
    return (
        rows % 64 == 0
        and LANES <= rows <= 2 * LANES
        and rows & (rows - 1) == 0
        and freq_count & (freq_count - 1) == 0
        and channels == 2**levels
        and rows % (freq_count * 2 * SUBLANES) == 0
        and freq_count >= 4
        and span % LANES == 0
        and channels - rows + LANES <= span
    )


def local(spectra, delays, widths):
    if fits(*spectra.shape, lax.axis_size("freq"), delays.shape[0]):
        return by_residues(spectra, delays, widths)
    return by_levels(spectra, delays, widths)


def solution(mesh):
    return jax.shard_map(
        local,
        mesh=mesh,
        in_specs=(P(("beam", "freq"), "tm"), P(), P()),
        out_specs=P(None, ("beam", "freq"), "tm"),
        check_vma=False,
    )
```

```python
import functools

import jax
import jax.numpy as jnp
from jax import lax
from jax.experimental import pallas as pl
from jax.experimental.pallas import tpu as pltpu
from jax.sharding import PartitionSpec as P

LANES = 128
SUBLANES = 8
TAPS = 128
LATER = 0.5
LOCAL_VMEM, CROSS_VMEM, FILTER_VMEM = 60 * 2**20, 24 * 2**20, 12 * 2**20


def lane_gather(block, index):
    return jnp.take_along_axis(block, index, axis=1, mode="promise_in_bounds")


def add_delayed(load_a, load_b, store, shifts, level, in_blocks, out_blocks):
    block_choices = max(1, 2**level // LANES)
    bits = block_choices.bit_length() - 1
    whole = jnp.minimum(shifts >> 7, block_choices - 1)
    reach = lax.broadcasted_iota(jnp.int32, shifts.shape, 1) + shifts - (whole << 7)
    index, stays = reach & (LANES - 1), reach < LANES
    wanted = [(whole & 2**bit) != 0 for bit in range(bits)]
    kept = {}

    def source(stage, j):
        if (stage, j) not in kept:
            if stage == 0:
                kept[stage, j] = load_b(j)
            else:
                later = source(stage - 1, j + 2 ** (stage - 1))
                kept[stage, j] = jnp.where(wanted[stage - 1], later, source(stage - 1, j))
        return kept[stage, j]

    def turned(j):
        if j + block_choices > in_blocks:
            return jnp.zeros((SUBLANES, LANES), jnp.float32)
        return lane_gather(source(bits, j), index)

    held = turned(0)
    for j in range(out_blocks):
        following = turned(j + 1)
        store(j, load_a(j) + jnp.where(stays, held, following))
        held = following


def block_of(j):
    return slice(j * LANES, (j + 1) * LANES)


def spread_shifts(table, spread, count, levels):
    per_step = max(n for n in (1, 2, 4) if count % n == 0)

    def step(item, carry):
        for e in range(per_step):
            tile = item * per_step + e
            values = table[pl.ds(pl.multiple_of(tile * SUBLANES, SUBLANES), SUBLANES), :]
            for n, level in enumerate(levels):
                spread[n, pl.ds(pl.multiple_of(tile * SUBLANES, SUBLANES), SUBLANES), :] = (
                    jnp.broadcast_to(values[:, level : level + 1], (SUBLANES, LANES))
                )
        return carry

    lax.fori_loop(0, count // per_step, step, 0)


def views(parts, count, mine, share):
    if len(parts) == 1:
        return [(parts[0], pl.ds(0, count))]
    return [
        (part, pl.ds(pl.multiple_of(jnp.bitwise_xor(mine, mask) * share, SUBLANES), share))
        for mask, part in enumerate(parts)
    ]


def local_tree_kernel(chunks, freq_count, place, spectra, rim, table, *refs):
    rows, span = spectra.shape
    levels = rows.bit_length() - 1
    outs, (even, odd, done, spread, held, in_sem, out_sem) = refs[:-7], refs[-7:]
    total, out_blocks = even.shape[0], span // LANES
    mine = place[0]
    own = table.at[pl.ds(pl.multiple_of(mine * rows, SUBLANES), rows), :]
    shifts = pltpu.make_async_copy(own, held, in_sem.at[total])
    loads = []
    for j in range(total):
        at = j - out_blocks
        source = rim.at[:, block_of(at)] if at >= 0 else spectra.at[:, block_of(j)]
        loads.append(pltpu.make_async_copy(source, even.at[j], in_sem.at[j]))
    for load in [shifts, *loads]:
        load.start()
    shifts.wait()
    spread_shifts(held, spread, rows // SUBLANES, range(levels))
    for load in loads:
        load.wait()
    pairs = rows // (2 * SUBLANES)
    per_step = max(n for n in (1, 2, 4, 8) if pairs % n == 0)
    for level in range(levels):
        half = 2**level
        last = level == levels - 1
        source, target = (even, odd) if level % 2 == 0 else (odd, even)

        def step(item, carry, level=level, half=half, last=last, source=source, target=target):
            for n in range(per_step):
                pair = item * per_step + n
                if half < SUBLANES:
                    group, member = pair // 4, pair % 4
                    start = group * 64 + (member // half) * 2 * half + member % half
                    spots = [
                        pl.ds(start + e * half, SUBLANES, stride=SUBLANES) for e in range(2)
                    ]
                else:
                    tiles = half // SUBLANES
                    tile = (pair // tiles) * 2 * tiles + pair % tiles
                    spots = [
                        pl.ds(pl.multiple_of((tile + e * tiles) * SUBLANES, SUBLANES), SUBLANES)
                        for e in range(2)
                    ]
                for spot in spots:

                    def put(j, value, spot=spot):
                        if last:
                            done[spot, block_of(j)] = value
                        else:
                            target[j, spot, :] = value

                    add_delayed(
                        lambda j: source[j, spots[0], :],
                        lambda j: source[j, spots[1], :],
                        put,
                        spread[level, spot, :],
                        level,
                        total,
                        out_blocks if last else total,
                    )
            return carry

        lax.fori_loop(0, pairs // per_step, step, 0)
    stores = []
    for start, count, parts in chunks:
        targets, outs = outs[:parts], outs[parts:]
        for target, spot in views(targets, count, mine, count // freq_count):
            source = done.at[pl.ds(start, count), :].at[spot, :]
            stores.append(pltpu.make_async_copy(source, target, out_sem.at[len(stores)]))
    for store in stores:
        store.start()
    for store in stores:
        store.wait()


def local_tree(position, spectra, rim, table, chunks, freq_count):
    count = sum(parts for _, _, parts in chunks)
    rows, span = spectra.shape
    total = (span + rim.shape[1]) // LANES
    hbm = pl.BlockSpec(memory_space=pl.ANY)
    return pl.pallas_call(
        functools.partial(local_tree_kernel, tuple(chunks), freq_count),
        out_shape=[
            jax.ShapeDtypeStruct((size // parts, span), jnp.float32)
            for _, size, parts in chunks
            for _ in range(parts)
        ],
        in_specs=[pl.BlockSpec(memory_space=pltpu.SMEM), hbm, hbm, hbm],
        out_specs=[pl.BlockSpec(memory_space=pltpu.HBM)] * count,
        scratch_shapes=[
            pltpu.VMEM((total, rows, LANES), jnp.float32),
            pltpu.VMEM((total, rows, LANES), jnp.float32),
            pltpu.VMEM((rows, span), jnp.float32),
            pltpu.VMEM((rows.bit_length() - 1, rows, LANES), jnp.int32),
            pltpu.VMEM((rows, LANES), jnp.int32),
            pltpu.SemaphoreType.DMA((total + 1,)),
            pltpu.SemaphoreType.DMA((count,)),
        ],
        compiler_params=pltpu.CompilerParams(vmem_limit_bytes=LOCAL_VMEM),
        cost_estimate=pl.CostEstimate(
            flops=8 * rows * span, bytes_accessed=8 * rows * span, transcendentals=0
        ),
        name="local_tree",
    )(position, spectra, rim, table)


def cross_tree_kernel(rows, freq_count, count, place, table, rim, *refs):
    parts, outs, refs = refs[:count], refs[count : 2 * count], refs[2 * count :]
    even, odd, done, spread, held, in_sem, out_sem = refs
    group, span = even.shape[0], parts[0].shape[1]
    share = group // freq_count
    blocks = even.shape[1] // LANES
    mine = place[0]
    loads = []
    loads.append(pltpu.make_async_copy(table, held, in_sem.at[0]))
    sources = [(0, pair) for pair in views(parts, group, mine, share)]
    edges = [rim] if count == 1 else [rim.at[n] for n in range(count)]
    sources += [(span, pair) for pair in views(edges, group, mine, share)]
    for start, (source, spot) in sources:
        target = even.at[spot, pl.ds(start, source.shape[1])]
        loads.append(pltpu.make_async_copy(source, target, in_sem.at[len(loads)]))
    for load in loads:
        load.start()
    loads[0].wait()
    first_level = rows.bit_length() - 1
    levels = freq_count.bit_length() - 1
    tiles = share // SUBLANES
    spread_shifts(held, spread, freq_count * tiles, range(first_level, first_level + levels))
    for load in loads[1:]:
        load.wait()
    items = freq_count // 2 * tiles
    per_step = 2 if items % 2 == 0 else 1
    for bit in range(levels):
        level = first_level + bit
        out_blocks = blocks - 2**level // LANES
        source, target = (even, odd) if bit % 2 == 0 else (odd, even)
        target = done if bit == levels - 1 else target

        def step(
            item, carry, bit=bit, level=level, blocks=blocks, out_blocks=out_blocks, source=source, target=target
        ):
            for n in range(per_step):
                pair, tile = (item * per_step + n) // tiles, (item * per_step + n) % tiles
                first = (pair // 2**bit) * 2 * 2**bit + pair % 2**bit
                spots = [
                    pl.ds(
                        pl.multiple_of((first + e * 2**bit) * share + tile * SUBLANES, SUBLANES),
                        SUBLANES,
                    )
                    for e in range(2)
                ]
                for spot in spots:

                    def put(j, value, spot=spot):
                        target[spot, block_of(j)] = value

                    add_delayed(
                        lambda j: source[spots[0], block_of(j)],
                        lambda j: source[spots[1], block_of(j)],
                        put,
                        spread[bit, spot, :],
                        level,
                        blocks,
                        out_blocks,
                    )
            return carry

        lax.fori_loop(0, items // per_step, step, 0)
        blocks = out_blocks
    stores = [
        pltpu.make_async_copy(done.at[spot, :], target, out_sem.at[n])
        for n, (target, spot) in enumerate(views(outs, group, mine, share))
    ]
    for store in stores:
        store.start()
    for store in stores:
        store.wait()


def cross_tree(position, table, parts, rim, rows, freq_count):
    count = len(parts)
    size, span = parts[0].shape
    group = size * count
    total = span + rim.shape[-1]
    hbm = pl.BlockSpec(memory_space=pl.ANY)
    return pl.pallas_call(
        functools.partial(cross_tree_kernel, rows, freq_count, count),
        out_shape=[jax.ShapeDtypeStruct((size, span + LANES), jnp.float32)] * count,
        in_specs=[pl.BlockSpec(memory_space=pltpu.SMEM)] + [hbm] * (2 + count),
        out_specs=[pl.BlockSpec(memory_space=pltpu.HBM if count == 1 else pl.ANY)] * count,
        scratch_shapes=[
            pltpu.VMEM((group, total), jnp.float32),
            pltpu.VMEM((group, total), jnp.float32),
            pltpu.VMEM((group, span + LANES), jnp.float32),
            pltpu.VMEM((freq_count.bit_length() - 1, group, LANES), jnp.int32),
            pltpu.VMEM((group, LANES), jnp.int32),
            pltpu.SemaphoreType.DMA((1 + 2 * count,)),
            pltpu.SemaphoreType.DMA((count,)),
        ],
        compiler_params=pltpu.CompilerParams(vmem_limit_bytes=CROSS_VMEM),
        cost_estimate=pl.CostEstimate(
            flops=4 * group * span, bytes_accessed=8 * group * span, transcendentals=0
        ),
        name="cross_tree",
    )(position, table, rim, *parts)


def filter_kernel(base, masks, place, widths, scale, earlier, *refs):
    out, mark, values, halves, before, whole, results, in_sem, out_sem = refs[-9:]
    mark[...] = jnp.zeros_like(mark)
    count, share = values.shape[:2]
    if masks:
        pieces = refs[:count]
        starts = [jnp.bitwise_xor(place[0], mask) * share for mask in masks]
    else:
        pieces = [refs[0].at[pl.ds(n * share, share), :] for n in range(count)]
        starts = [n * share for n in range(count)]
    blocks = out.shape[2] // LANES
    filters = out.shape[0]
    loads = [pltpu.make_async_copy(pieces[n], values.at[n], in_sem.at[n]) for n in range(count)]
    for load in loads:
        load.start()
    row = lax.broadcasted_iota(jnp.int32, (2 * LANES, 2 * LANES), 0) & (LANES - 1)
    col = lax.broadcasted_iota(jnp.int32, (2 * LANES, 2 * LANES), 1)
    ones = ((row < col) | (col >= LANES)).astype(jnp.bfloat16)
    per_dot = max(n for n in (1, 2, 3, 4, 5, 6, 7) if (blocks + 1) % n == 0)
    lane = lax.broadcasted_iota(jnp.int32, (SUBLANES, LANES), 1)
    copies = {}
    for n in range(count):
        slot = n % 2
        loads[n].wait()
        for j in range(blocks + 1):
            exact = values[n, :, block_of(j)]
            high = exact.astype(jnp.bfloat16)
            low = (exact - high.astype(jnp.float32)).astype(jnp.bfloat16)
            halves[j, :, pl.ds(0, LANES)] = high
            halves[j, :, pl.ds(LANES, LANES)] = low
        for item in range((blocks + 1) // per_dot):
            taken = halves[item * per_dot : (item + 1) * per_dot]
            product = jnp.dot(
                taken.reshape(per_dot * share, 2 * LANES), ones, preferred_element_type=jnp.float32
            )
            for e in range(per_dot):
                rows = slice(e * share, (e + 1) * share)
                before[item * per_dot + e] = product[rows, :LANES]
                whole[item * per_dot + e] = product[rows, LANES:]
        if n >= 2:
            for copy in copies[n - 2]:
                copy.wait()

        def step(item, carry, slot=slot):
            which, tile = item // (share // SUBLANES), item % (share // SUBLANES)
            width = widths[which]
            factor = scale[which]
            stays = lane < LANES - width
            at = pl.ds(pl.multiple_of(tile * SUBLANES, SUBLANES), SUBLANES)
            first = before[0, at, :]
            turned = pltpu.roll(first, LANES - width, 1)
            for j in range(blocks):
                second = before[j + 1, at, :]
                following = pltpu.roll(second, LANES - width, 1)
                upper = jnp.where(stays, turned, following + whole[j, at, :])
                results[slot, which, at, block_of(j)] = (upper - first) * factor
                first, turned = second, following
            return carry

        lax.fori_loop(0, filters * share // SUBLANES, step, 0, unroll=8)
        copies[n] = [
            pltpu.make_async_copy(
                results.at[slot, which],
                out.at[which, pl.ds(pl.multiple_of(base + starts[n], SUBLANES), share), :],
                out_sem.at[slot, which],
            )
            for which in range(filters)
        ]
        for copy in copies[n]:
            copy.start()
    for n in range(max(0, count - 2), count):
        for copy in copies[n]:
            copy.wait()


def box_filters(position, widths, scale, earlier, parts, masks, result, rows, base):
    size, reach = parts[0].shape
    share = size if masks else max(n for n in (16, 32) if size % n == 0)
    count = len(parts) * size // share
    span = reach - LANES
    blocks = span // LANES
    filters = scale.shape[0]
    hbm = pl.BlockSpec(memory_space=pl.ANY)
    smem = pl.BlockSpec(memory_space=pltpu.SMEM)
    operands = [position, widths, scale, earlier, *parts]
    aliases = {}
    if result is not None:
        aliases = {len(operands): 0}
        operands.append(result)
    return pl.pallas_call(
        functools.partial(filter_kernel, base, tuple(masks)),
        out_shape=[
            jax.ShapeDtypeStruct((filters, rows, span), jnp.float32),
            jax.ShapeDtypeStruct((SUBLANES, LANES), jnp.float32),
        ],
        in_specs=[smem] * 3 + [hbm] * (len(operands) - 3),
        out_specs=[hbm, pl.BlockSpec(memory_space=pltpu.VMEM)],
        input_output_aliases=aliases,
        scratch_shapes=[
            pltpu.VMEM((count, share, reach), jnp.float32),
            pltpu.VMEM((blocks + 1, share, 2 * LANES), jnp.bfloat16),
            pltpu.VMEM((blocks + 1, share, LANES), jnp.float32),
            pltpu.VMEM((blocks + 1, share, LANES), jnp.float32),
            pltpu.VMEM((2, filters, share, span), jnp.float32),
            pltpu.SemaphoreType.DMA((count,)),
            pltpu.SemaphoreType.DMA((2, filters)),
        ],
        compiler_params=pltpu.CompilerParams(vmem_limit_bytes=FILTER_VMEM),
        cost_estimate=pl.CostEstimate(
            flops=8 * count * share * span * filters,
            bytes_accessed=4 * count * share * span * (filters + 1),
            transcendentals=0,
        ),
        name="box_filters",
    )(*operands)


def passed_along(value, axis, steps):
    count = lax.axis_size(axis)
    initial, last = (max(0, -steps), min(count, count - steps))
    return lax.ppermute(value, axis, [(source, source + steps) for source in range(initial, last)])


def exchanged(parts, freq_count):
    if len(parts) == 1:
        return [lax.all_to_all(parts[0], "freq", 0, 0, tiled=True)]
    result = list(parts)
    for mask in range(1, freq_count):
        pairs = [(source, source ^ mask) for source in range(freq_count)]
        result[mask] = lax.ppermute(parts[mask], "freq", pairs)
    return result


def chunks_of(rows, freq_count):
    tiles = rows // freq_count // SUBLANES
    first = tiles - max(1, int(tiles * LATER))
    counts = [first * SUBLANES * freq_count, (tiles - first) * SUBLANES * freq_count]
    return [(0, counts[0], freq_count), (counts[0], counts[1], 1)]


def by_residues(spectra, delays, widths):
    rows, span = spectra.shape
    freq_count = lax.axis_size("freq")
    channels = rows * freq_count
    position = lax.axis_index("freq").astype(jnp.int32)[None]
    local_rim = -(-(rows - 1) // LANES) * LANES
    rim = passed_along(spectra[:, :local_rim], "tm", -1)
    table = jnp.pad(delays.T, ((0, 0), (0, LANES - delays.shape[0])))
    scale = 1.0 / jnp.sqrt(widths.astype(jnp.float32) * channels)
    reach = channels - rows + LANES
    chunks = chunks_of(rows, freq_count)
    made = local_tree(position, spectra, rim, table, chunks, freq_count)
    tables = {}
    for base, size, _ in chunks:
        share = size // freq_count
        mine = lax.dynamic_slice_in_dim(
            table.reshape(freq_count, rows, LANES), base + position[0] * share, share, axis=1
        )
        tables[base] = mine.reshape(size, LANES)
    arrived = []
    for _, _, count in chunks:
        arrived.append(exchanged(made[:count], freq_count))
        made = made[count:]
    back = []
    for (base, _, count), parts in zip(chunks, arrived):
        edges = [part[:, :reach] for part in parts]
        rim = passed_along(jnp.stack(edges) if count > 1 else edges[0], "tm", -1)
        back.append(cross_tree(position, tables[base], parts, rim, rows, freq_count))
    back = [exchanged(parts, freq_count) for parts in back]
    result, mark = None, jnp.zeros((SUBLANES, LANES), jnp.float32)
    half = freq_count // 2
    turns = [(0, range(half)), (1, ()), (0, range(half, freq_count - 2))]
    turns += [(0, (mask,)) for mask in range(freq_count - 2, freq_count)]
    for chunk, masks in turns:
        base, parts = chunks[chunk][0], back[chunk]
        some = [parts[mask] for mask in masks] or parts
        result, mark = box_filters(
            position, widths, scale, mark, some, tuple(masks), result, rows, base
        )
    return result


def from_partner(value, axis, stride):
    mask = 2**stride
    pairs = [(source, source ^ mask) for source in range(lax.axis_size(axis))]
    return lax.ppermute(value, axis, pairs)


def delay_rows(source_rows, row_shifts, out_width):
    total_width = source_rows.shape[1]
    top_reach = total_width - out_width
    shift_col = row_shifts[:, None]
    low_part = shift_col % top_reach
    result = source_rows
    bit_value = 1
    while bit_value < top_reach:
        width_now = result.shape[1]
        chosen = low_part // bit_value % 2 == 1
        result = jnp.where(chosen, result[:, bit_value:], result[:, : width_now - bit_value])
        bit_value = bit_value * 2
    lower_shift = result[:, :out_width]
    top_shift = source_rows[:, top_reach : top_reach + out_width]
    return jnp.where(shift_col == top_reach, top_shift, lower_shift)


def delay_block(current, row_shifts, half_rows, out_width):
    row_count, total_width = current.shape
    group_count = row_count // (2 * half_rows)
    block_view = current.reshape(group_count, 2, half_rows, total_width)
    source_rows = jnp.broadcast_to(
        block_view[:, 1][:, None], (group_count, 2, half_rows, total_width)
    )
    delayed = delay_rows(source_rows.reshape(row_count, total_width), row_shifts, out_width)
    summed = block_view[:, 0, :, :out_width][:, None] + delayed.reshape(
        group_count, 2, half_rows, out_width
    )
    return summed.reshape(row_count, out_width)


def by_levels(spectra, delays, widths):
    row_count, time_span = spectra.shape
    local_levels = row_count.bit_length() - 1
    freq_count = lax.axis_size("freq")
    cross_levels = freq_count.bit_length() - 1
    position = lax.axis_index("freq")

    def own_shifts(tree_level):
        return lax.dynamic_slice_in_dim(delays[tree_level], position * row_count, row_count)

    current = spectra
    rim_depth = 2**local_levels - 1
    leading = passed_along(current[:, :rim_depth], "tm", -1)
    current = jnp.concatenate([current, leading], axis=1)
    for tree_level in range(local_levels):
        current = delay_block(
            current, own_shifts(tree_level), 2**tree_level, current.shape[1] - 2**tree_level
        )
    for bit_index in range(cross_levels):
        tree_level = local_levels + bit_index
        reach = 2**tree_level
        leading = passed_along(current[:, :reach], "tm", -1)
        own_ext = jnp.concatenate([current, leading], axis=1)
        partner_ext = from_partner(own_ext, "freq", bit_index)
        is_lower = position // 2**bit_index % 2 == 0
        first_term = jnp.where(is_lower, own_ext[:, :time_span], partner_ext[:, :time_span])
        second_source = jnp.where(is_lower, partner_ext, own_ext)
        current = first_term + delay_rows(second_source, own_shifts(tree_level), time_span)
    leading = passed_along(current[:, :TAPS], "tm", -1)
    extended = jnp.concatenate([current, leading], axis=1)
    block_count = time_span // TAPS
    block_view = extended.reshape(row_count, block_count + 1, TAPS)
    paired = jnp.concatenate([block_view[:, :-1], block_view[:, 1:]], axis=2)
    filter_count = widths.shape[0]
    input_pos = lax.broadcasted_iota(jnp.int32, (2 * TAPS, filter_count, TAPS), 0)
    output_pos = lax.broadcasted_iota(jnp.int32, (2 * TAPS, filter_count, TAPS), 2)
    distance = input_pos - output_pos
    box_widths = widths[None, :, None]
    scaling = 1.0 / jnp.sqrt(widths.astype(jnp.float32) * (row_count * freq_count))
    filter_matrix = jnp.where(
        (distance >= 0) & (distance < box_widths), scaling[None, :, None], 0.0
    )
    filter_matrix = filter_matrix.reshape(2 * TAPS, filter_count * TAPS)
    product = jnp.einsum("rbj,jk->rbk", paired, filter_matrix, precision=lax.Precision.HIGHEST)
    product = product.reshape(row_count, block_count, filter_count, TAPS)
    return jnp.transpose(product, (2, 0, 1, 3)).reshape(filter_count, row_count, time_span)


def fits(rows, span, freq_count, levels):
    channels = rows * freq_count
    return (
        rows % 64 == 0
        and LANES <= rows <= 2 * LANES
        and rows & (rows - 1) == 0
        and freq_count & (freq_count - 1) == 0
        and channels == 2**levels
        and rows % (freq_count * 2 * SUBLANES) == 0
        and freq_count >= 4
        and span % LANES == 0
        and channels - rows + LANES <= span
    )


def local(spectra, delays, widths):
    if fits(*spectra.shape, lax.axis_size("freq"), delays.shape[0]):
        return by_residues(spectra, delays, widths)
    return by_levels(spectra, delays, widths)


def solution(mesh):
    return jax.shard_map(
        local,
        mesh=mesh,
        in_specs=(P(("beam", "freq"), "tm"), P(), P()),
        out_specs=P(None, ("beam", "freq"), "tm"),
        check_vma=False,
    )
```

```python
import functools

import jax
import jax.numpy as jnp
from jax import lax
from jax.experimental import pallas as pl
from jax.experimental.pallas import tpu as pltpu
from jax.sharding import PartitionSpec as P

LANES = 128
SUBLANES = 8
TAPS = 128
LATER = 0.5
LOCAL_VMEM, CROSS_VMEM, FILTER_VMEM = 60 * 2**20, 24 * 2**20, 12 * 2**20


def lane_gather(block, index):
    return jnp.take_along_axis(block, index, axis=1, mode="promise_in_bounds")


def add_delayed(load_a, load_b, store, shifts, level, in_blocks, out_blocks):
    block_choices = max(1, 2**level // LANES)
    bits = block_choices.bit_length() - 1
    whole = jnp.minimum(shifts >> 7, block_choices - 1)
    reach = lax.broadcasted_iota(jnp.int32, shifts.shape, 1) + shifts - (whole << 7)
    index, stays = reach & (LANES - 1), reach < LANES
    wanted = [(whole & 2**bit) != 0 for bit in range(bits)]
    kept = {}

    def source(stage, j):
        if (stage, j) not in kept:
            if stage == 0:
                kept[stage, j] = load_b(j)
            else:
                later = source(stage - 1, j + 2 ** (stage - 1))
                kept[stage, j] = jnp.where(wanted[stage - 1], later, source(stage - 1, j))
        return kept[stage, j]

    def turned(j):
        if j + block_choices > in_blocks:
            return jnp.zeros((SUBLANES, LANES), jnp.float32)
        return lane_gather(source(bits, j), index)

    held = turned(0)
    for j in range(out_blocks):
        following = turned(j + 1)
        store(j, load_a(j) + jnp.where(stays, held, following))
        held = following


def block_of(j):
    return slice(j * LANES, (j + 1) * LANES)


def spread_shifts(table, spread, count, levels):
    per_step = max(n for n in (1, 2, 4) if count % n == 0)

    def step(item, carry):
        for e in range(per_step):
            tile = item * per_step + e
            values = table[pl.ds(pl.multiple_of(tile * SUBLANES, SUBLANES), SUBLANES), :]
            for n, level in enumerate(levels):
                spread[n, pl.ds(pl.multiple_of(tile * SUBLANES, SUBLANES), SUBLANES), :] = (
                    jnp.broadcast_to(values[:, level : level + 1], (SUBLANES, LANES))
                )
        return carry

    lax.fori_loop(0, count // per_step, step, 0)


def views(parts, count, mine, share):
    if len(parts) == 1:
        return [(parts[0], pl.ds(0, count))]
    return [
        (part, pl.ds(pl.multiple_of(jnp.bitwise_xor(mine, mask) * share, SUBLANES), share))
        for mask, part in enumerate(parts)
    ]


def local_tree_kernel(chunks, freq_count, place, spectra, rim, table, *refs):
    rows, span = spectra.shape
    levels = rows.bit_length() - 1
    outs, (even, odd, done, spread, held, in_sem, out_sem) = refs[:-7], refs[-7:]
    total, out_blocks = even.shape[0], span // LANES
    mine = place[0]
    own = table.at[pl.ds(pl.multiple_of(mine * rows, SUBLANES), rows), :]
    shifts = pltpu.make_async_copy(own, held, in_sem.at[total])
    loads = []
    for j in range(total):
        at = j - out_blocks
        source = rim.at[:, block_of(at)] if at >= 0 else spectra.at[:, block_of(j)]
        loads.append(pltpu.make_async_copy(source, even.at[j], in_sem.at[j]))
    for load in [shifts, *loads]:
        load.start()
    shifts.wait()
    spread_shifts(held, spread, rows // SUBLANES, range(levels))
    for load in loads:
        load.wait()
    pairs = rows // (2 * SUBLANES)
    per_step = max(n for n in (1, 2, 4, 8) if pairs % n == 0)
    for level in range(levels):
        half = 2**level
        last = level == levels - 1
        source, target = (even, odd) if level % 2 == 0 else (odd, even)

        def step(item, carry, level=level, half=half, last=last, source=source, target=target):
            for n in range(per_step):
                pair = item * per_step + n
                if half < SUBLANES:
                    group, member = pair // 4, pair % 4
                    start = group * 64 + (member // half) * 2 * half + member % half
                    spots = [
                        pl.ds(start + e * half, SUBLANES, stride=SUBLANES) for e in range(2)
                    ]
                else:
                    tiles = half // SUBLANES
                    tile = (pair // tiles) * 2 * tiles + pair % tiles
                    spots = [
                        pl.ds(pl.multiple_of((tile + e * tiles) * SUBLANES, SUBLANES), SUBLANES)
                        for e in range(2)
                    ]
                for spot in spots:

                    def put(j, value, spot=spot):
                        if last:
                            done[spot, block_of(j)] = value
                        else:
                            target[j, spot, :] = value

                    add_delayed(
                        lambda j: source[j, spots[0], :],
                        lambda j: source[j, spots[1], :],
                        put,
                        spread[level, spot, :],
                        level,
                        total,
                        out_blocks if last else total,
                    )
            return carry

        lax.fori_loop(0, pairs // per_step, step, 0)
    stores = []
    for start, count, parts in chunks:
        targets, outs = outs[:parts], outs[parts:]
        for target, spot in views(targets, count, mine, count // freq_count):
            source = done.at[pl.ds(start, count), :].at[spot, :]
            stores.append(pltpu.make_async_copy(source, target, out_sem.at[len(stores)]))
    for store in stores:
        store.start()
    for store in stores:
        store.wait()


def local_tree(position, spectra, rim, table, chunks, freq_count):
    count = sum(parts for _, _, parts in chunks)
    rows, span = spectra.shape
    total = (span + rim.shape[1]) // LANES
    hbm = pl.BlockSpec(memory_space=pl.ANY)
    return pl.pallas_call(
        functools.partial(local_tree_kernel, tuple(chunks), freq_count),
        out_shape=[
            jax.ShapeDtypeStruct((size // parts, span), jnp.float32)
            for _, size, parts in chunks
            for _ in range(parts)
        ],
        in_specs=[pl.BlockSpec(memory_space=pltpu.SMEM), hbm, hbm, hbm],
        out_specs=[pl.BlockSpec(memory_space=pltpu.HBM)] * count,
        scratch_shapes=[
            pltpu.VMEM((total, rows, LANES), jnp.float32),
            pltpu.VMEM((total, rows, LANES), jnp.float32),
            pltpu.VMEM((rows, span), jnp.float32),
            pltpu.VMEM((rows.bit_length() - 1, rows, LANES), jnp.int32),
            pltpu.VMEM((rows, LANES), jnp.int32),
            pltpu.SemaphoreType.DMA((total + 1,)),
            pltpu.SemaphoreType.DMA((count,)),
        ],
        compiler_params=pltpu.CompilerParams(vmem_limit_bytes=LOCAL_VMEM),
        cost_estimate=pl.CostEstimate(
            flops=8 * rows * span, bytes_accessed=8 * rows * span, transcendentals=0
        ),
        name="local_tree",
    )(position, spectra, rim, table)


def cross_tree_kernel(rows, freq_count, count, place, table, rim, *refs):
    parts, outs, refs = refs[:count], refs[count : 2 * count], refs[2 * count :]
    even, odd, done, spread, held, in_sem, out_sem = refs
    group, span = even.shape[0], parts[0].shape[1]
    share = group // freq_count
    blocks = even.shape[1] // LANES
    mine = place[0]
    loads = []
    loads.append(pltpu.make_async_copy(table, held, in_sem.at[0]))
    sources = [(0, pair) for pair in views(parts, group, mine, share)]
    edges = [rim] if count == 1 else [rim.at[n] for n in range(count)]
    sources += [(span, pair) for pair in views(edges, group, mine, share)]
    for start, (source, spot) in sources:
        target = even.at[spot, pl.ds(start, source.shape[1])]
        loads.append(pltpu.make_async_copy(source, target, in_sem.at[len(loads)]))
    for load in loads:
        load.start()
    loads[0].wait()
    first_level = rows.bit_length() - 1
    levels = freq_count.bit_length() - 1
    tiles = share // SUBLANES
    spread_shifts(held, spread, freq_count * tiles, range(first_level, first_level + levels))
    for load in loads[1:]:
        load.wait()
    items = freq_count // 2 * tiles
    per_step = 2 if items % 2 == 0 else 1
    for bit in range(levels):
        level = first_level + bit
        out_blocks = blocks - 2**level // LANES
        source, target = (even, odd) if bit % 2 == 0 else (odd, even)
        target = done if bit == levels - 1 else target

        def step(
            item, carry, bit=bit, level=level, blocks=blocks, out_blocks=out_blocks, source=source, target=target
        ):
            for n in range(per_step):
                pair, tile = (item * per_step + n) // tiles, (item * per_step + n) % tiles
                first = (pair // 2**bit) * 2 * 2**bit + pair % 2**bit
                spots = [
                    pl.ds(
                        pl.multiple_of((first + e * 2**bit) * share + tile * SUBLANES, SUBLANES),
                        SUBLANES,
                    )
                    for e in range(2)
                ]
                for spot in spots:

                    def put(j, value, spot=spot):
                        target[spot, block_of(j)] = value

                    add_delayed(
                        lambda j: source[spots[0], block_of(j)],
                        lambda j: source[spots[1], block_of(j)],
                        put,
                        spread[bit, spot, :],
                        level,
                        blocks,
                        out_blocks,
                    )
            return carry

        lax.fori_loop(0, items // per_step, step, 0)
        blocks = out_blocks
    stores = [
        pltpu.make_async_copy(done.at[spot, :], target, out_sem.at[n])
        for n, (target, spot) in enumerate(views(outs, group, mine, share))
    ]
    for store in stores:
        store.start()
    for store in stores:
        store.wait()


def cross_tree(position, table, parts, rim, rows, freq_count, width):
    count = len(parts)
    size, span = parts[0].shape
    group = size * count
    total = span + rim.shape[-1]
    hbm = pl.BlockSpec(memory_space=pl.ANY)
    return pl.pallas_call(
        functools.partial(cross_tree_kernel, rows, freq_count, count),
        out_shape=[jax.ShapeDtypeStruct((size, width), jnp.float32)] * count,
        in_specs=[pl.BlockSpec(memory_space=pltpu.SMEM)] + [hbm] * (2 + count),
        out_specs=[pl.BlockSpec(memory_space=pltpu.HBM if count == 1 else pl.ANY)] * count,
        scratch_shapes=[
            pltpu.VMEM((group, total), jnp.float32),
            pltpu.VMEM((group, total), jnp.float32),
            pltpu.VMEM((group, width), jnp.float32),
            pltpu.VMEM((freq_count.bit_length() - 1, group, LANES), jnp.int32),
            pltpu.VMEM((group, LANES), jnp.int32),
            pltpu.SemaphoreType.DMA((1 + 2 * count,)),
            pltpu.SemaphoreType.DMA((count,)),
        ],
        compiler_params=pltpu.CompilerParams(vmem_limit_bytes=CROSS_VMEM),
        cost_estimate=pl.CostEstimate(
            flops=4 * group * span, bytes_accessed=8 * group * span, transcendentals=0
        ),
        name="cross_tree",
    )(position, table, rim, *parts)


def filter_kernel(base, masks, place, widths, scale, earlier, *refs):
    out, mark, values, halves, before, whole, results, in_sem, out_sem = refs[-9:]
    mark[...] = jnp.zeros_like(mark)
    count, share = values.shape[:2]
    if masks:
        pieces = refs[:count]
        starts = [jnp.bitwise_xor(place[0], mask) * share for mask in masks]
    else:
        pieces, edges = [
            [ref.at[pl.ds(n * share, share), :] for n in range(count)] for ref in refs[:2]
        ]
        starts = [n * share for n in range(count)]
    blocks = out.shape[2] // LANES
    filters = out.shape[0]
    loads = []
    for n in range(count):
        whole_piece = values.at[n]
        if not masks:
            whole_piece = values.at[n, :, pl.ds(0, blocks * LANES)]
            edge = values.at[n, :, pl.ds(blocks * LANES, LANES)]
            pltpu.make_async_copy(edges[n], edge, in_sem.at[count + n]).start()
        loads.append(pltpu.make_async_copy(pieces[n], whole_piece, in_sem.at[n]))
        loads[n].start()
    row = lax.broadcasted_iota(jnp.int32, (2 * LANES, 2 * LANES), 0) & (LANES - 1)
    col = lax.broadcasted_iota(jnp.int32, (2 * LANES, 2 * LANES), 1)
    ones = ((row < col) | (col >= LANES)).astype(jnp.bfloat16)
    per_dot = max(n for n in (1, 2, 3, 4, 5, 6, 7) if (blocks + 1) % n == 0)
    lane = lax.broadcasted_iota(jnp.int32, (SUBLANES, LANES), 1)
    copies = {}
    for n in range(count):
        slot = n % 2
        loads[n].wait()
        if not masks:
            edge = values.at[n, :, pl.ds(blocks * LANES, LANES)]
            pltpu.make_async_copy(edges[n], edge, in_sem.at[count + n]).wait()
        for j in range(blocks + 1):
            exact = values[n, :, block_of(j)]
            high = exact.astype(jnp.bfloat16)
            low = (exact - high.astype(jnp.float32)).astype(jnp.bfloat16)
            halves[j, :, pl.ds(0, LANES)] = high
            halves[j, :, pl.ds(LANES, LANES)] = low
        for item in range((blocks + 1) // per_dot):
            taken = halves[item * per_dot : (item + 1) * per_dot]
            product = jnp.dot(
                taken.reshape(per_dot * share, 2 * LANES), ones, preferred_element_type=jnp.float32
            )
            for e in range(per_dot):
                rows = slice(e * share, (e + 1) * share)
                before[item * per_dot + e] = product[rows, :LANES]
                whole[item * per_dot + e] = product[rows, LANES:]
        if n >= 2:
            for copy in copies[n - 2]:
                copy.wait()

        def step(item, carry, slot=slot):
            which, tile = item // (share // SUBLANES), item % (share // SUBLANES)
            width = widths[which]
            factor = scale[which]
            stays = lane < LANES - width
            at = pl.ds(pl.multiple_of(tile * SUBLANES, SUBLANES), SUBLANES)
            first = before[0, at, :]
            turned = pltpu.roll(first, LANES - width, 1)
            for j in range(blocks):
                second = before[j + 1, at, :]
                following = pltpu.roll(second, LANES - width, 1)
                upper = jnp.where(stays, turned, following + whole[j, at, :])
                results[slot, which, at, block_of(j)] = (upper - first) * factor
                first, turned = second, following
            return carry

        lax.fori_loop(0, filters * share // SUBLANES, step, 0, unroll=8)
        copies[n] = [
            pltpu.make_async_copy(
                results.at[slot, which],
                out.at[which, pl.ds(pl.multiple_of(base + starts[n], SUBLANES), share), :],
                out_sem.at[slot, which],
            )
            for which in range(filters)
        ]
        for copy in copies[n]:
            copy.start()
    for n in range(max(0, count - 2), count):
        for copy in copies[n]:
            copy.wait()


def box_filters(position, widths, scale, earlier, parts, masks, edge, result, rows, base):
    size, reach = parts[0].shape
    reach += LANES if edge is not None else 0
    share = size if masks else max(n for n in (16, 32) if size % n == 0)
    count = len(parts) * size // share
    span = reach - LANES
    blocks = span // LANES
    filters = scale.shape[0]
    hbm = pl.BlockSpec(memory_space=pl.ANY)
    smem = pl.BlockSpec(memory_space=pltpu.SMEM)
    operands = [position, widths, scale, earlier, *parts]
    operands += [] if edge is None else [edge]
    aliases = {}
    if result is not None:
        aliases = {len(operands): 0}
        operands.append(result)
    return pl.pallas_call(
        functools.partial(filter_kernel, base, tuple(masks)),
        out_shape=[
            jax.ShapeDtypeStruct((filters, rows, span), jnp.float32),
            jax.ShapeDtypeStruct((SUBLANES, LANES), jnp.float32),
        ],
        in_specs=[smem] * 3 + [hbm] * (len(operands) - 3),
        out_specs=[hbm, pl.BlockSpec(memory_space=pltpu.VMEM)],
        input_output_aliases=aliases,
        scratch_shapes=[
            pltpu.VMEM((count, share, reach), jnp.float32),
            pltpu.VMEM((blocks + 1, share, 2 * LANES), jnp.bfloat16),
            pltpu.VMEM((blocks + 1, share, LANES), jnp.float32),
            pltpu.VMEM((blocks + 1, share, LANES), jnp.float32),
            pltpu.VMEM((2, filters, share, span), jnp.float32),
            pltpu.SemaphoreType.DMA((2 * count,)),
            pltpu.SemaphoreType.DMA((2, filters)),
        ],
        compiler_params=pltpu.CompilerParams(vmem_limit_bytes=FILTER_VMEM),
        cost_estimate=pl.CostEstimate(
            flops=8 * count * share * span * filters,
            bytes_accessed=4 * count * share * span * (filters + 1),
            transcendentals=0,
        ),
        name="box_filters",
    )(*operands)


def passed_along(value, axis, steps):
    count = lax.axis_size(axis)
    initial, last = (max(0, -steps), min(count, count - steps))
    return lax.ppermute(value, axis, [(source, source + steps) for source in range(initial, last)])


def exchanged(parts, freq_count):
    if len(parts) == 1:
        return [lax.all_to_all(parts[0], "freq", 0, 0, tiled=True)]
    result = list(parts)
    for mask in range(1, freq_count):
        pairs = [(source, source ^ mask) for source in range(freq_count)]
        result[mask] = lax.ppermute(parts[mask], "freq", pairs)
    return result


def chunks_of(rows, freq_count):
    tiles = rows // freq_count // SUBLANES
    first = tiles - max(1, int(tiles * LATER))
    counts = [first * SUBLANES * freq_count, (tiles - first) * SUBLANES * freq_count]
    return [(0, counts[0], freq_count), (counts[0], counts[1], 1)]


def by_residues(spectra, delays, widths):
    rows, span = spectra.shape
    freq_count = lax.axis_size("freq")
    channels = rows * freq_count
    position = lax.axis_index("freq").astype(jnp.int32)[None]
    local_rim = -(-(rows - 1) // LANES) * LANES
    rim = passed_along(spectra[:, :local_rim], "tm", -1)
    table = jnp.pad(delays.T, ((0, 0), (0, LANES - delays.shape[0])))
    scale = 1.0 / jnp.sqrt(widths.astype(jnp.float32) * channels)
    chunks = chunks_of(rows, freq_count)
    made = local_tree(position, spectra, rim, table, chunks, freq_count)
    tables = {}
    for base, size, _ in chunks:
        share = size // freq_count
        mine = lax.dynamic_slice_in_dim(
            table.reshape(freq_count, rows, LANES), base + position[0] * share, share, axis=1
        )
        tables[base] = mine.reshape(size, LANES)
    arrived = []
    for _, _, count in chunks:
        arrived.append(exchanged(made[:count], freq_count))
        made = made[count:]
    back = []
    for (base, _, count), parts in zip(chunks, arrived):
        extra = LANES if count > 1 else 0
        edges = [part[:, : channels - rows + extra] for part in parts]
        rim = passed_along(jnp.stack(edges) if count > 1 else edges[0], "tm", -1)
        back.append(cross_tree(position, tables[base], parts, rim, rows, freq_count, span + extra))
    back = [exchanged(parts, freq_count) for parts in back]
    edge = passed_along(back[1][0][:, :LANES], "tm", -1)
    result, mark = None, jnp.zeros((SUBLANES, LANES), jnp.float32)
    half = freq_count // 2
    turns = [(0, range(half)), (1, ()), (0, range(half, freq_count - 2))]
    turns += [(0, (mask,)) for mask in range(freq_count - 2, freq_count)]
    for chunk, masks in turns:
        base, parts = chunks[chunk][0], back[chunk]
        some = [parts[mask] for mask in masks] or parts
        result, mark = box_filters(
            position,
            widths,
            scale,
            mark,
            some,
            tuple(masks),
            None if masks else edge,
            result,
            rows,
            base,
        )
    return result


def from_partner(value, axis, stride):
    mask = 2**stride
    pairs = [(source, source ^ mask) for source in range(lax.axis_size(axis))]
    return lax.ppermute(value, axis, pairs)


def delay_rows(source_rows, row_shifts, out_width):
    total_width = source_rows.shape[1]
    top_reach = total_width - out_width
    shift_col = row_shifts[:, None]
    low_part = shift_col % top_reach
    result = source_rows
    bit_value = 1
    while bit_value < top_reach:
        width_now = result.shape[1]
        chosen = low_part // bit_value % 2 == 1
        result = jnp.where(chosen, result[:, bit_value:], result[:, : width_now - bit_value])
        bit_value = bit_value * 2
    lower_shift = result[:, :out_width]
    top_shift = source_rows[:, top_reach : top_reach + out_width]
    return jnp.where(shift_col == top_reach, top_shift, lower_shift)


def delay_block(current, row_shifts, half_rows, out_width):
    row_count, total_width = current.shape
    group_count = row_count // (2 * half_rows)
    block_view = current.reshape(group_count, 2, half_rows, total_width)
    source_rows = jnp.broadcast_to(
        block_view[:, 1][:, None], (group_count, 2, half_rows, total_width)
    )
    delayed = delay_rows(source_rows.reshape(row_count, total_width), row_shifts, out_width)
    summed = block_view[:, 0, :, :out_width][:, None] + delayed.reshape(
        group_count, 2, half_rows, out_width
    )
    return summed.reshape(row_count, out_width)


def by_levels(spectra, delays, widths):
    row_count, time_span = spectra.shape
    local_levels = row_count.bit_length() - 1
    freq_count = lax.axis_size("freq")
    cross_levels = freq_count.bit_length() - 1
    position = lax.axis_index("freq")

    def own_shifts(tree_level):
        return lax.dynamic_slice_in_dim(delays[tree_level], position * row_count, row_count)

    current = spectra
    rim_depth = 2**local_levels - 1
    leading = passed_along(current[:, :rim_depth], "tm", -1)
    current = jnp.concatenate([current, leading], axis=1)
    for tree_level in range(local_levels):
        current = delay_block(
            current, own_shifts(tree_level), 2**tree_level, current.shape[1] - 2**tree_level
        )
    for bit_index in range(cross_levels):
        tree_level = local_levels + bit_index
        reach = 2**tree_level
        leading = passed_along(current[:, :reach], "tm", -1)
        own_ext = jnp.concatenate([current, leading], axis=1)
        partner_ext = from_partner(own_ext, "freq", bit_index)
        is_lower = position // 2**bit_index % 2 == 0
        first_term = jnp.where(is_lower, own_ext[:, :time_span], partner_ext[:, :time_span])
        second_source = jnp.where(is_lower, partner_ext, own_ext)
        current = first_term + delay_rows(second_source, own_shifts(tree_level), time_span)
    leading = passed_along(current[:, :TAPS], "tm", -1)
    extended = jnp.concatenate([current, leading], axis=1)
    block_count = time_span // TAPS
    block_view = extended.reshape(row_count, block_count + 1, TAPS)
    paired = jnp.concatenate([block_view[:, :-1], block_view[:, 1:]], axis=2)
    filter_count = widths.shape[0]
    input_pos = lax.broadcasted_iota(jnp.int32, (2 * TAPS, filter_count, TAPS), 0)
    output_pos = lax.broadcasted_iota(jnp.int32, (2 * TAPS, filter_count, TAPS), 2)
    distance = input_pos - output_pos
    box_widths = widths[None, :, None]
    scaling = 1.0 / jnp.sqrt(widths.astype(jnp.float32) * (row_count * freq_count))
    filter_matrix = jnp.where(
        (distance >= 0) & (distance < box_widths), scaling[None, :, None], 0.0
    )
    filter_matrix = filter_matrix.reshape(2 * TAPS, filter_count * TAPS)
    product = jnp.einsum("rbj,jk->rbk", paired, filter_matrix, precision=lax.Precision.HIGHEST)
    product = product.reshape(row_count, block_count, filter_count, TAPS)
    return jnp.transpose(product, (2, 0, 1, 3)).reshape(filter_count, row_count, time_span)


def fits(rows, span, freq_count, levels):
    channels = rows * freq_count
    return (
        rows % 64 == 0
        and LANES <= rows <= 2 * LANES
        and rows & (rows - 1) == 0
        and freq_count & (freq_count - 1) == 0
        and channels == 2**levels
        and rows % (freq_count * 2 * SUBLANES) == 0
        and freq_count >= 4
        and span % LANES == 0
        and channels - rows + LANES <= span
    )


def local(spectra, delays, widths):
    if fits(*spectra.shape, lax.axis_size("freq"), delays.shape[0]):
        return by_residues(spectra, delays, widths)
    return by_levels(spectra, delays, widths)


def solution(mesh):
    return jax.shard_map(
        local,
        mesh=mesh,
        in_specs=(P(("beam", "freq"), "tm"), P(), P()),
        out_specs=P(None, ("beam", "freq"), "tm"),
        check_vma=False,
    )
```
